128 devices in a mesh: rep: 2 (over core), grp: 64 (over z, y, x).
Axes of the slice: x: 4, y: 4, z: 4, core: 2. Of those that a mesh axis runs over, the one named last changes fastest.
Arguments:
- grad_parts: float32 [2, 1024, 9216], P('rep', 'grp'), may hold values from -6 to 6
- gain_grad_parts: float32 [2, 2, 1024], P('rep', None, 'grp'), may hold values from -6 to 6
- weights: float32 [1024, 9216], P('grp'), may hold values from -0.1875 to 0.1875
- basis: float32 [1024, 256], P('grp'), may hold values from -0.1875 to 0.1875
- moment_first: float32 [9216, 256], P('grp'), may hold values from -12 to 12
- moment_second: float32 [9216, 256], P('grp'), may hold values from 0.01 to 1
- gains: float32 [2, 1024], P(None, 'grp'), may hold values from 0.5 to 1.5
- gain_first: float32 [2, 1024], P(None, 'grp'), may hold values from -12 to 12
- gain_second: float32 [2, 1024], P(None, 'grp'), may hold values from 0.01 to 1
Outputs:
- new_weights: float32 [1024, 9216], P('grp')
- new_first: float32 [9216, 256], P('grp')
- new_second: float32 [9216, 256], P('grp')
- new_basis: float32 [1024, 256], P('grp')
- new_gains: float32 [2, 1024], P(None, 'grp')
- new_gain_first: float32 [2, 1024], P(None, 'grp')
- new_gain_second: float32 [2, 1024], P(None, 'grp')
The draws below stay inside these ranges and needn't reach their ends.
All inputs are finite; a program needn't handle non-finite values.
Results may differ from the reference program's by a relative error of at most 0.0001.
Values sent between devices are 32-bit elements; how exact they have to be, the bound alone decides.
No kernel may reach another device: no remote copies, remote signals or barrier semaphores. Data moves between devices by JAX's collectives and lax.ppermute only.
A program may use at most 64 MiB of HBM per device.

```python
import math
import jax
import jax.numpy as jnp
from jax import lax

D = 1024
RANK = 256
NS_STEPS = 3
NCOL = 9216
N_REP = 2


def shard_levels(own_key, shape, cuts, smallest, top_value):
    loudness, own = 1.0, jax.random.fold_in(own_key, 6)
    for axis_at, blocks in cuts:
        draws = jnp.exp(jax.random.uniform(jax.random.fold_in(own, axis_at), (blocks,), jnp.float32, smallest / len(cuts), top_value / len(cuts)))
        loudness = loudness * jnp.repeat(draws, shape[axis_at] // blocks).reshape([-1 if axis == axis_at else 1 for axis in range(len(shape))])
    return loudness


def bell_draw(rng, shape, deviation, limit, cuts=(), dtype=jnp.bfloat16):
    result = jax.random.normal(rng, shape, jnp.float32) * deviation
    if len(cuts) > 0:
        result = shard_levels(rng, shape, cuts, -0.22, 0.18) * result
    return jnp.clip(result, min=-limit, max=limit).astype(dtype)


def setup_inputs(seed: int = 0) -> dict:
    seeds = jax.random.split(jax.random.key(seed), 10)
    return {
        "grad_parts": bell_draw(seeds[0], (N_REP, D, NCOL), 1.0, 6.0, ((0, 2), (1, 64)), jnp.float32),
        "gain_grad_parts": bell_draw(seeds[1], (N_REP, 2, D), 1.0, 6.0, ((0, 2), (2, 64)), jnp.float32),
        "weights": bell_draw(seeds[2], (D, NCOL), D ** -0.5, 0.1875, ((0, 64),), jnp.float32),
        "basis": bell_draw(seeds[3], (D, RANK), D ** -0.5, 0.1875, ((0, 64),), jnp.float32),
        "moment_first": bell_draw(seeds[4], (NCOL, RANK), 2.0, 12.0, ((0, 64),), jnp.float32),
        "moment_second": jnp.clip(jnp.exp(math.log(1.0) - 4.6051702 * jax.random.uniform(seeds[5], (NCOL, RANK), jnp.float32) ** shard_levels(seeds[5], (NCOL, RANK), ((0, 64),), -0.2, 0.2)), 0.01, 1.0),
        "gains": jnp.clip(1.0 + 0.1 * jax.random.normal(seeds[6], (2, D), jnp.float32), 0.5, 1.5),
        "gain_first": bell_draw(seeds[7], (2, D), 2.0, 12.0, ((1, 64),), jnp.float32),
        "gain_second": jnp.clip(jnp.exp(math.log(1.0) - 4.6051702 * jax.random.uniform(seeds[8], (2, D), jnp.float32) ** shard_levels(seeds[8], (2, D), ((1, 64),), -0.2, 0.2)), 0.01, 1.0),
    }


beta_first = 0.9
beta_second = 0.999
learn_rate = 0.1
galore_scale = 0.25
adam_eps = 1e-08

def exact_dot(left, right):
    return jnp.dot(left, right, precision=lax.Precision.HIGHEST, preferred_element_type=jnp.float32)

def reference(grad_parts, gain_grad_parts, weights, basis, moment_first, moment_second, gains, gain_first, gain_second):
    corr_first = 1.0 - beta_first ** 10
    corr_second = 1.0 - beta_second ** 10
    grad = lax.optimization_barrier(jnp.sum(grad_parts, axis=0))
    gain_grad = lax.optimization_barrier(jnp.sum(gain_grad_parts, axis=0))
    projected = exact_dot(grad.T, basis)
    new_first = beta_first * moment_first + (1.0 - beta_first) * projected
    new_second = beta_second * moment_second + (1.0 - beta_second) * projected * projected
    direction = new_first / corr_first / (jnp.sqrt(new_second / corr_second) + adam_eps)
    new_weights = weights - learn_rate * galore_scale * exact_dot(basis, direction.T)
    subspace = exact_dot(grad, projected)
    gram = exact_dot(subspace.T, subspace)
    scale = jnp.sqrt(jnp.sqrt(jnp.sum(gram * gram) + 1e-06))
    iterate = subspace / scale
    for step in range(NS_STEPS):
        iterate = 1.5 * iterate - 0.5 * exact_dot(iterate, exact_dot(iterate.T, iterate))
    new_gain_first = beta_first * gain_first + (1.0 - beta_first) * gain_grad
    new_gain_second = beta_second * gain_second + (1.0 - beta_second) * gain_grad * gain_grad
    new_gains = gains - learn_rate * (new_gain_first / corr_first) / (jnp.sqrt(new_gain_second / corr_second) + adam_eps)
    return (new_weights, new_first, new_second, iterate, new_gains, new_gain_first, new_gain_second)
```

```python
import functools

import jax
import jax.numpy as jnp
from jax import lax
from jax.experimental import pallas as pl
from jax.experimental.pallas import tpu as pltpu
from jax.sharding import PartitionSpec as P

NS_STEPS = 3

beta_first = 0.9
beta_second = 0.999
learn_rate = 0.1
galore_scale = 0.25
adam_eps = 1e-08

CHIPS = 64
ROWS = 8
NCOL = 9216
OWN = NCOL // CHIPS
WIN = 256
RANK = 256
LANE = 128
VMEM_LIMIT = 56 * 1024 * 1024

SWAP = [(0, 1), (1, 0)]


def window_start(chip):
    return (OWN * chip) // LANE * LANE


def dot(left, right, left_dim, right_dim):
    return lax.dot_general(
        left,
        right,
        (((left_dim,), (right_dim,)), ((), ())),
        precision=lax.Precision.HIGHEST,
        preferred_element_type=jnp.float32,
    )


def call(kernel, out_shape, scratch=()):
    return pl.pallas_call(
        kernel,
        out_shape=out_shape,
        scratch_shapes=list(scratch),
        compiler_params=pltpu.CompilerParams(vmem_limit_bytes=VMEM_LIMIT),
    )


def f32(*shape):
    return jax.ShapeDtypeStruct(shape, jnp.float32)


def pack_kernel(own_ref, other_ref, basis_ref, out_ref):
    half = pl.ds(pl.multiple_of(lax.axis_index("rep") * ROWS, ROWS), ROWS)
    rows = basis_ref[half, :]
    for chip in range(CHIPS):
        cols = pl.ds(window_start(chip), WIN)
        out_ref[chip, :, :WIN] = own_ref[half, cols] + other_ref[half, cols]
        out_ref[chip, :, WIN:] = rows


def own_rows():
    return pl.ds(pl.multiple_of(lax.rem(lax.axis_index("grp"), 8) * 16, 16), OWN)


def project_kernel(in_ref, out_ref, scratch):
    scratch[...] = dot(in_ref[:, :WIN], in_ref[:, WIN:], 0, 0)
    out_ref[...] = scratch[own_rows(), :]


def adam_kernel(
    in_ref, own_ref, other_ref, first_ref, second_ref,
    out_ref, new_first_ref, new_second_ref, projected_win, direction_win,
):
    corr_first = 1.0 - beta_first**10
    corr_second = 1.0 - beta_second**10
    projected = own_ref[...] + other_ref[...]
    new_first = beta_first * first_ref[...] + (1.0 - beta_first) * projected
    new_second = beta_second * second_ref[...] + (1.0 - beta_second) * projected * projected
    new_first_ref[...] = new_first
    new_second_ref[...] = new_second
    direction = new_first / corr_first / (jnp.sqrt(new_second / corr_second) + adam_eps)
    projected_win[...] = jnp.zeros_like(projected_win)
    direction_win[...] = jnp.zeros_like(direction_win)
    projected_win[own_rows(), :] = projected
    direction_win[own_rows(), :] = direction
    out_ref[:, :RANK] = dot(in_ref[:, :WIN], projected_win[...], 1, 0)
    out_ref[:, RANK:] = dot(in_ref[:, WIN:], direction_win[...], 1, 1)


def subspace_kernel(in_ref, rows_ref, out_ref):
    rows = jnp.sum(in_ref[:, :, :RANK], axis=0)
    rows_ref[...] = rows
    out_ref[...] = jnp.broadcast_to(rows[None], out_ref.shape)


def weights_kernel(in_ref, weights_ref, out_ref):
    half = pl.ds(pl.multiple_of(lax.axis_index("rep") * ROWS, ROWS), ROWS)
    tiles = {}
    for chip in range(CHIPS):
        tile = window_start(chip) // LANE
        for part in range(2):
            tiles.setdefault(tile + part, []).append((chip, RANK + part * LANE))
    for tile, terms in tiles.items():
        total = sum(in_ref[chip, :, pl.ds(at, LANE)] for chip, at in terms)
        cols = pl.ds(tile * LANE, LANE)
        out_ref[:, cols] = weights_ref[half, cols] - learn_rate * galore_scale * total


def join_kernel(own_ref, other_ref, out_ref):
    core = lax.axis_index("rep")
    out_ref[pl.ds(pl.multiple_of(core * ROWS, ROWS), ROWS), :] = own_ref[...]
    out_ref[pl.ds(pl.multiple_of((1 - core) * ROWS, ROWS), ROWS), :] = other_ref[...]


def gram_kernel(in_ref, out_ref):
    subspace = in_ref[...]
    out_ref[...] = dot(subspace, subspace, 0, 0)


def refresh_kernel(own_gram_ref, other_gram_ref, rows_ref, other_rows_ref, out_ref):
    core = lax.axis_index("rep")
    gram = own_gram_ref[...] + other_gram_ref[...]
    scale = jnp.sqrt(jnp.sqrt(jnp.sum(gram * gram, keepdims=True) + 1e-06))
    iterate = jnp.concatenate([rows_ref[...], other_rows_ref[...]], axis=0) / scale
    current = gram / scale / scale
    diagonal = lax.broadcasted_iota(jnp.int32, (RANK, RANK), 0) == lax.broadcasted_iota(
        jnp.int32, (RANK, RANK), 1
    )
    for step in range(NS_STEPS):
        factor = jnp.where(diagonal, 1.5, 0.0) - 0.5 * current
        iterate = dot(iterate, factor, 1, 0)
        if step + 1 < NS_STEPS:
            current = dot(dot(factor, current, 1, 0), factor, 1, 0)
    out_ref[pl.ds(pl.multiple_of(core * ROWS, ROWS), ROWS), :] = iterate[:ROWS]
    out_ref[pl.ds(pl.multiple_of((1 - core) * ROWS, ROWS), ROWS), :] = iterate[ROWS:]


def body(
    grad_parts,
    gain_grad_parts,
    weights,
    basis,
    moment_first,
    moment_second,
    gains,
    gain_first,
    gain_second,
):
    corr_first = 1.0 - beta_first**10
    corr_second = 1.0 - beta_second**10
    swap = functools.partial(lax.ppermute, axis_name="rep", perm=SWAP)
    exchange = functools.partial(
        lax.all_to_all, axis_name="grp", split_axis=0, concat_axis=0, tiled=True
    )
    local_grad = grad_parts[0]
    local_gain = gain_grad_parts[0]
    packed = call(pack_kernel, f32(CHIPS, ROWS, WIN + RANK))(local_grad, swap(local_grad), basis)
    block = exchange(packed).reshape(CHIPS * ROWS, WIN + RANK)
    part = call(project_kernel, f32(OWN, RANK), [pltpu.VMEM((WIN, RANK), jnp.float32)])(block)
    out, new_first, new_second = call(
        adam_kernel,
        (f32(CHIPS * ROWS, 2 * RANK), f32(OWN, RANK), f32(OWN, RANK)),
        [pltpu.VMEM((WIN, RANK), jnp.float32)] * 2,
    )(block, part, swap(part), moment_first, moment_second)
    back = exchange(out.reshape(CHIPS, ROWS, 2 * RANK))
    rows, spread = call(subspace_kernel, (f32(ROWS, RANK), f32(CHIPS, ROWS, RANK)))(back)
    subspace = exchange(spread).reshape(CHIPS * ROWS, RANK)
    half = call(weights_kernel, f32(ROWS, NCOL))(back, weights)
    new_weights = call(join_kernel, f32(2 * ROWS, NCOL))(half, swap(half))
    gram = call(gram_kernel, f32(RANK, RANK))(subspace)
    iterate = call(refresh_kernel, f32(2 * ROWS, RANK))(gram, swap(gram), rows, swap(rows))

    gain_grad = local_gain + swap(local_gain)
    new_gain_first = beta_first * gain_first + (1.0 - beta_first) * gain_grad
    new_gain_second = beta_second * gain_second + (1.0 - beta_second) * gain_grad * gain_grad
    new_gains = gains - learn_rate * (new_gain_first / corr_first) / (
        jnp.sqrt(new_gain_second / corr_second) + adam_eps
    )
    return (new_weights, new_first, new_second, iterate, new_gains, new_gain_first, new_gain_second)


def solution(mesh):
    in_specs = (
        P("rep", "grp", None),
        P("rep", None, "grp"),
        P("grp", None),
        P("grp", None),
        P("grp", None),
        P("grp", None),
        P(None, "grp"),
        P(None, "grp"),
        P(None, "grp"),
    )
    out_specs = (
        P("grp", None),
        P("grp", None),
        P("grp", None),
        P("grp", None),
        P(None, "grp"),
        P(None, "grp"),
        P(None, "grp"),
    )
    return jax.shard_map(body, mesh=mesh, in_specs=in_specs, out_specs=out_specs, check_vma=False)
```

```python
import functools

import jax
import jax.numpy as jnp
from jax import lax
from jax.experimental import pallas as pl
from jax.experimental.pallas import tpu as pltpu
from jax.sharding import PartitionSpec as P

NS_STEPS = 3

beta_first = 0.9
beta_second = 0.999
learn_rate = 0.1
galore_scale = 0.25
adam_eps = 1e-08

CHIPS = 64
ROWS = 8
NCOL = 9216
OWN = NCOL // CHIPS
WIN = 256
RANK = 256
LANE = 128
VMEM_LIMIT = 16 * 1024 * 1024

SWAP = [(0, 1), (1, 0)]


def window_start(chip):
    return (OWN * chip) // LANE * LANE


def dot(left, right, left_dim, right_dim):
    return lax.dot_general(
        left,
        right,
        (((left_dim,), (right_dim,)), ((), ())),
        precision=lax.Precision.HIGHEST,
        preferred_element_type=jnp.float32,
    )


def call(kernel, out_shape, scratch=()):
    return pl.pallas_call(
        kernel,
        out_shape=out_shape,
        scratch_shapes=list(scratch),
        compiler_params=pltpu.CompilerParams(vmem_limit_bytes=VMEM_LIMIT),
    )


def f32(*shape):
    return jax.ShapeDtypeStruct(shape, jnp.float32)


def pack_kernel(own_ref, other_ref, basis_ref, out_ref):
    half = pl.ds(pl.multiple_of(lax.axis_index("rep") * ROWS, ROWS), ROWS)
    rows = basis_ref[half, :]
    for chip in range(CHIPS):
        cols = pl.ds(window_start(chip), WIN)
        out_ref[chip, :, :WIN] = own_ref[half, cols] + other_ref[half, cols]
        out_ref[chip, :, WIN:] = rows


def own_rows():
    return pl.ds(pl.multiple_of(lax.rem(lax.axis_index("grp"), 8) * 16, 16), OWN)


def project_kernel(in_ref, out_ref, scratch):
    scratch[...] = dot(in_ref[:, :WIN], in_ref[:, WIN:], 0, 0)
    out_ref[...] = scratch[own_rows(), :]


def adam_kernel(
    in_ref, own_ref, other_ref, first_ref, second_ref,
    out_ref, new_first_ref, new_second_ref, projected_win, direction_win,
):
    corr_first = 1.0 - beta_first**10
    corr_second = 1.0 - beta_second**10
    projected = own_ref[...] + other_ref[...]
    new_first = beta_first * first_ref[...] + (1.0 - beta_first) * projected
    new_second = beta_second * second_ref[...] + (1.0 - beta_second) * projected * projected
    new_first_ref[...] = new_first
    new_second_ref[...] = new_second
    direction = new_first / corr_first / (jnp.sqrt(new_second / corr_second) + adam_eps)
    projected_win[...] = jnp.zeros_like(projected_win)
    direction_win[...] = jnp.zeros_like(direction_win)
    projected_win[own_rows(), :] = projected
    direction_win[own_rows(), :] = direction
    out_ref[:, :RANK] = dot(in_ref[:, :WIN], projected_win[...], 1, 0)
    out_ref[:, RANK:] = dot(in_ref[:, WIN:], direction_win[...], 1, 1)


def subspace_kernel(in_ref, rows_ref, out_ref):
    rows = jnp.sum(in_ref[:, :, :RANK], axis=0)
    rows_ref[...] = rows
    out_ref[...] = jnp.broadcast_to(rows[None], out_ref.shape)


def weights_kernel(in_ref, weights_ref, out_ref):
    half = pl.ds(pl.multiple_of(lax.axis_index("rep") * ROWS, ROWS), ROWS)
    tiles = {}
    for chip in range(CHIPS):
        tile = window_start(chip) // LANE
        for part in range(2):
            tiles.setdefault(tile + part, []).append((chip, RANK + part * LANE))
    for tile, terms in tiles.items():
        total = sum(in_ref[chip, :, pl.ds(at, LANE)] for chip, at in terms)
        cols = pl.ds(tile * LANE, LANE)
        out_ref[:, cols] = weights_ref[half, cols] - learn_rate * galore_scale * total


def join_kernel(own_ref, other_ref, out_ref):
    core = lax.axis_index("rep")
    out_ref[pl.ds(pl.multiple_of(core * ROWS, ROWS), ROWS), :] = own_ref[...]
    out_ref[pl.ds(pl.multiple_of((1 - core) * ROWS, ROWS), ROWS), :] = other_ref[...]


def gram_kernel(in_ref, out_ref):
    subspace = in_ref[...]
    out_ref[...] = dot(subspace, subspace, 0, 0)


def refresh_kernel(own_gram_ref, other_gram_ref, rows_ref, other_rows_ref, out_ref):
    core = lax.axis_index("rep")
    gram = own_gram_ref[...] + other_gram_ref[...]
    scale = jnp.sqrt(jnp.sqrt(jnp.sum(gram * gram, keepdims=True) + 1e-06))
    iterate = jnp.concatenate([rows_ref[...], other_rows_ref[...]], axis=0) / scale
    current = gram / scale / scale
    diagonal = lax.broadcasted_iota(jnp.int32, (RANK, RANK), 0) == lax.broadcasted_iota(
        jnp.int32, (RANK, RANK), 1
    )
    for step in range(NS_STEPS):
        factor = jnp.where(diagonal, 1.5, 0.0) - 0.5 * current
        iterate = dot(iterate, factor, 1, 0)
        if step + 1 < NS_STEPS:
            current = dot(dot(factor, current, 1, 0), factor, 1, 0)
    out_ref[pl.ds(pl.multiple_of(core * ROWS, ROWS), ROWS), :] = iterate[:ROWS]
    out_ref[pl.ds(pl.multiple_of((1 - core) * ROWS, ROWS), ROWS), :] = iterate[ROWS:]


def body(
    grad_parts,
    gain_grad_parts,
    weights,
    basis,
    moment_first,
    moment_second,
    gains,
    gain_first,
    gain_second,
):
    corr_first = 1.0 - beta_first**10
    corr_second = 1.0 - beta_second**10
    swap = functools.partial(lax.ppermute, axis_name="rep", perm=SWAP)
    exchange = functools.partial(
        lax.all_to_all, axis_name="grp", split_axis=0, concat_axis=0, tiled=True
    )
    local_grad = grad_parts[0]
    local_gain = gain_grad_parts[0]
    packed = call(pack_kernel, f32(CHIPS, ROWS, WIN + RANK))(local_grad, swap(local_grad), basis)
    block = exchange(packed).reshape(CHIPS * ROWS, WIN + RANK)
    part = call(project_kernel, f32(OWN, RANK), [pltpu.VMEM((WIN, RANK), jnp.float32)])(block)
    out, new_first, new_second = call(
        adam_kernel,
        (f32(CHIPS * ROWS, 2 * RANK), f32(OWN, RANK), f32(OWN, RANK)),
        [pltpu.VMEM((WIN, RANK), jnp.float32)] * 2,
    )(block, part, swap(part), moment_first, moment_second)
    back = exchange(out.reshape(CHIPS, ROWS, 2 * RANK))
    rows, spread = call(subspace_kernel, (f32(ROWS, RANK), f32(CHIPS, ROWS, RANK)))(back)
    subspace = exchange(spread).reshape(CHIPS * ROWS, RANK)
    half = call(weights_kernel, f32(ROWS, NCOL))(back, weights)
    new_weights = call(join_kernel, f32(2 * ROWS, NCOL))(half, swap(half))
    gram = call(gram_kernel, f32(RANK, RANK))(subspace)
    iterate = call(refresh_kernel, f32(2 * ROWS, RANK))(gram, swap(gram), rows, swap(rows))

    gain_grad = local_gain + swap(local_gain)
    new_gain_first = beta_first * gain_first + (1.0 - beta_first) * gain_grad
    new_gain_second = beta_second * gain_second + (1.0 - beta_second) * gain_grad * gain_grad
    new_gains = gains - learn_rate * (new_gain_first / corr_first) / (
        jnp.sqrt(new_gain_second / corr_second) + adam_eps
    )
    return (new_weights, new_first, new_second, iterate, new_gains, new_gain_first, new_gain_second)


def solution(mesh):
    in_specs = (
        P("rep", "grp", None),
        P("rep", None, "grp"),
        P("grp", None),
        P("grp", None),
        P("grp", None),
        P("grp", None),
        P(None, "grp"),
        P(None, "grp"),
        P(None, "grp"),
    )
    out_specs = (
        P("grp", None),
        P("grp", None),
        P("grp", None),
        P("grp", None),
        P(None, "grp"),
        P(None, "grp"),
        P(None, "grp"),
    )
    return jax.shard_map(body, mesh=mesh, in_specs=in_specs, out_specs=out_specs, check_vma=False)
```

```python
import functools

import jax
import jax.numpy as jnp
from jax import lax
from jax.experimental import pallas as pl
from jax.experimental.pallas import tpu as pltpu
from jax.sharding import PartitionSpec as P

NS_STEPS = 3

beta_first = 0.9
beta_second = 0.999
learn_rate = 0.1
galore_scale = 0.25
adam_eps = 1e-08

CHIPS = 64
ROWS = 8
NCOL = 9216
OWN = NCOL // CHIPS
RANK = 256
LANE = 128
PIECE = 16
BLOCK = 25
VMEM_LIMIT = 16 * 1024 * 1024

SWAP = [(0, 1), (1, 0)]


def dot(left, right, left_dim, right_dim):
    return lax.dot_general(
        left,
        right,
        (((left_dim,), (right_dim,)), ((), ())),
        precision=lax.Precision.HIGHEST,
        preferred_element_type=jnp.float32,
    )


def call(kernel, out_shape, scratch=(), **specs):
    return pl.pallas_call(
        kernel,
        out_shape=out_shape,
        **specs,
        scratch_shapes=list(scratch),
        compiler_params=pltpu.CompilerParams(vmem_limit_bytes=VMEM_LIMIT),
    )


def f32(*shape):
    return jax.ShapeDtypeStruct(shape, jnp.float32)


def any_spec():
    return pl.BlockSpec(memory_space=pl.ANY)


def vmem_spec():
    return pl.BlockSpec(memory_space=pltpu.VMEM)


def iota(axis):
    return lax.broadcasted_iota(jnp.int32, (ROWS, LANE), axis)


def half_rows(core):
    return pl.ds(pl.multiple_of(core * ROWS, ROWS), ROWS)


def swap_pieces(tile):
    row, piece = iota(0), iota(1) // PIECE
    for bit in (1, 2, 4):
        up = pltpu.roll(pltpu.roll(tile, ROWS - bit, 0), PIECE * bit, 1)
        down = pltpu.roll(pltpu.roll(tile, bit, 0), LANE - PIECE * bit, 1)
        row_set, piece_set = (row & bit) != 0, (piece & bit) != 0
        tile = jnp.where(row_set == piece_set, tile, jnp.where(piece_set, up, down))
    return tile


def octet(group):
    return pl.ds(BLOCK * 8 * group + BLOCK - 1, 8, stride=BLOCK)


def stage_kernel(grad_ref, basis_ref, grad_out, basis_out):
    half = half_rows(lax.axis_index("rep"))
    grad_out[...] = grad_ref[half, :]
    basis_out[...] = basis_ref[half, :]


def pack_kernel(own_ref, other_ref, basis_ref, out_ref):
    half = half_rows(lax.axis_index("rep"))
    lane, piece = iota(1), iota(1) // PIECE
    low, high = basis_ref[:, :LANE], basis_ref[:, LANE:]
    for group in range(8):
        tiles = []
        for t in range(9):
            cols = pl.ds((9 * group + t) * LANE, LANE)
            tiles.append(own_ref[:, cols] + other_ref[half, cols])
        last = tiles[8]
        for j in range(8):
            at = BLOCK * (8 * group + j)
            out_ref[at : at + 8, :] = jnp.where(lane >= PIECE * j, tiles[j], tiles[j + 1])
            out_ref[at + 8 : at + 16, :] = low
            out_ref[at + 16 : at + 24, :] = high
            last = jnp.where(piece == j, tiles[j + 1], last)
        out_ref[octet(group), :] = swap_pieces(last)


def project_kernel(in_ref, grad_ref, basis_ref, out_ref, twice):
    piece = iota(1) // PIECE
    for group in range(8):
        last = swap_pieces(in_ref[octet(group), :])
        for j in range(8):
            chip = 8 * group + j
            at, rows = BLOCK * chip, slice(ROWS * chip, ROWS * chip + ROWS)
            grad_ref[rows, :LANE] = in_ref[at : at + 8, :]
            grad_ref[rows, LANE:] = jnp.where(piece == j, last, 0.0)
            basis_ref[rows, :LANE] = in_ref[at + 8 : at + 16, :]
            basis_ref[rows, LANE:] = in_ref[at + 16 : at + 24, :]
    product = dot(grad_ref[...], basis_ref[...], 0, 0)
    twice[:LANE, :] = product[:LANE]
    twice[LANE:, :] = product[:LANE]
    first = pl.multiple_of(lax.rem(lax.axis_index("grp"), 8) * PIECE, PIECE)
    out_ref[:LANE, :] = twice[pl.ds(first, LANE), :]
    out_ref[LANE:, :] = sum(
        product[LANE + PIECE * j : LANE + PIECE * (j + 1)] for j in range(8)
    )


def spread_columns(values, twice, out):
    twice[:LANE, :] = values[:LANE]
    twice[LANE:, :] = values[:LANE]
    first = pl.multiple_of(LANE - lax.rem(lax.axis_index("grp"), 8) * PIECE, PIECE)
    out[:LANE, :] = twice[pl.ds(first, LANE), :]
    for j in range(8):
        out[LANE + PIECE * j : LANE + PIECE * (j + 1), :] = values[LANE:]


def adam(value, first, second):
    corr_first = 1.0 - beta_first**10
    corr_second = 1.0 - beta_second**10
    new_first = beta_first * first + (1.0 - beta_first) * value
    new_second = beta_second * second + (1.0 - beta_second) * value * value
    direction = new_first / corr_first / (jnp.sqrt(new_second / corr_second) + adam_eps)
    return new_first, new_second, direction


def adam_kernel(
    grad_ref, basis_ref, own_ref, other_ref, first_ref, second_ref,
    gain_own_ref, gain_other_ref, gains_ref, gain_first_ref, gain_second_ref,
    out_ref, new_first_ref, new_second_ref, new_gains_ref, new_gain_first_ref, new_gain_second_ref,
    twice, projected_wide, direction_wide,
):
    projected = own_ref[...] + other_ref[...]
    new_first, new_second, direction = adam(projected, first_ref[...], second_ref[...])
    new_first_ref[...] = new_first
    new_second_ref[...] = new_second
    spread_columns(projected, twice, projected_wide)
    spread_columns(direction, twice, direction_wide)
    subspace = dot(grad_ref[...], projected_wide[...], 1, 0)
    update = dot(basis_ref[...], direction_wide[...], 1, 1)
    diagonal = iota(0) == iota(1) // PIECE
    for chip in range(CHIPS):
        at, rows = BLOCK * chip, slice(ROWS * chip, ROWS * chip + ROWS)
        out_ref[at : at + 8, :] = update[rows, :LANE]
        out_ref[at + 8 : at + 16, :] = subspace[rows, :LANE]
        out_ref[at + 16 : at + 24, :] = subspace[rows, LANE:]
        out_ref[at + 24 : at + 25, :] = jnp.sum(
            jnp.where(diagonal, update[rows, LANE:], 0.0), axis=0, keepdims=True
        )
    gain_grad = gain_own_ref[...] + gain_other_ref[...]
    new_first, new_second, direction = adam(gain_grad, gain_first_ref[...], gain_second_ref[...])
    new_gain_first_ref[...] = new_first
    new_gain_second_ref[...] = new_second
    new_gains_ref[...] = gains_ref[...] - learn_rate * direction


def subspace_kernel(in_ref, rows_ref, out_ref):
    low = sum(in_ref[BLOCK * chip + 8 : BLOCK * chip + 16, :] for chip in range(CHIPS))
    high = sum(in_ref[BLOCK * chip + 16 : BLOCK * chip + 24, :] for chip in range(CHIPS))
    rows = jnp.concatenate([low, high], axis=1)
    rows_ref[...] = rows
    out_ref[...] = jnp.broadcast_to(rows[None], out_ref.shape)


def weights_kernel(in_ref, weights_ref, out_ref):
    half = half_rows(lax.axis_index("rep"))
    lane = iota(1)
    for group in range(8):
        last = swap_pieces(in_ref[octet(group), :])
        mains = [
            in_ref[BLOCK * (8 * group + j) : BLOCK * (8 * group + j) + 8, :] for j in range(8)
        ]
        for t in range(9):
            update = last
            if t < 8:
                update = jnp.where(lane >= PIECE * t, mains[t], update)
            if t > 0:
                update = jnp.where(lane < PIECE * (t - 1), mains[t - 1], update)
            cols = pl.ds((9 * group + t) * LANE, LANE)
            out_ref[:, cols] = weights_ref[half, cols] - learn_rate * galore_scale * update


def join_kernel(own_ref, other_ref, rows_ref, other_rows_ref, out_ref, rows_out):
    core = lax.axis_index("rep")
    out_ref[half_rows(core), :] = own_ref[...]
    out_ref[half_rows(1 - core), :] = other_ref[...]
    rows_out[half_rows(core), :] = rows_ref[...]
    rows_out[half_rows(1 - core), :] = other_rows_ref[...]


def gram_kernel(in_ref, rows_ref, out_ref):
    subspace = in_ref[...]
    out_ref[...] = dot(subspace, subspace, 0, 0)


def refresh_kernel(own_gram_ref, other_gram_ref, rows_ref, out_ref):
    gram = own_gram_ref[...] + other_gram_ref[...]
    scale = jnp.sqrt(jnp.sqrt(jnp.sum(gram * gram, keepdims=True) + 1e-06))
    iterate = rows_ref[...] / scale
    current = gram / scale / scale
    diagonal = lax.broadcasted_iota(jnp.int32, (RANK, RANK), 0) == lax.broadcasted_iota(
        jnp.int32, (RANK, RANK), 1
    )
    for step in range(NS_STEPS):
        factor = jnp.where(diagonal, 1.5, 0.0) - 0.5 * current
        iterate = dot(iterate, factor, 1, 0)
        if step + 1 < NS_STEPS:
            current = dot(dot(factor, current, 1, 0), factor, 1, 0)
    out_ref[...] = iterate


def body(
    grad_parts,
    gain_grad_parts,
    weights,
    basis,
    moment_first,
    moment_second,
    gains,
    gain_first,
    gain_second,
):
    swap = functools.partial(lax.ppermute, axis_name="rep", perm=SWAP)
    vmem = pltpu.VMEM

    def exchange(blocks):
        out = lax.all_to_all(blocks, "grp", split_axis=0, concat_axis=0, tiled=True)
        return out

    def exchange_blocks(blocks):
        return exchange(blocks.reshape(CHIPS * BLOCK, 1, LANE)).reshape(CHIPS * BLOCK, LANE)

    wide = f32(CHIPS * ROWS, RANK)
    local_grad = grad_parts[0]
    local_gain = gain_grad_parts[0]
    other_grad = swap(local_grad)
    other_gain = swap(local_gain)
    own_grad, own_basis = call(stage_kernel, (f32(ROWS, NCOL), f32(ROWS, RANK)))(local_grad, basis)
    packed = call(pack_kernel, f32(CHIPS * BLOCK, LANE))(own_grad, other_grad, own_basis)
    columns, full_basis, part = call(
        project_kernel, (wide, wide, f32(OWN, RANK)), [vmem((2 * LANE, RANK), jnp.float32)]
    )(exchange_blocks(packed))
    small = f32(2, 2 * ROWS)
    out, new_first, new_second, new_gains, new_gain_first, new_gain_second = call(
        adam_kernel,
        (f32(CHIPS * BLOCK, LANE), f32(OWN, RANK), f32(OWN, RANK), small, small, small),
        [vmem((2 * LANE, RANK), jnp.float32)] * 3,
    )(
        columns, full_basis, part, swap(part), moment_first, moment_second,
        local_gain, other_gain, gains, gain_first, gain_second,
    )
    back = exchange_blocks(out)
    rows, spread = call(subspace_kernel, (f32(ROWS, RANK), f32(CHIPS, ROWS, RANK)))(back)
    subspace = exchange(spread).reshape(CHIPS * ROWS, RANK)
    half = call(weights_kernel, f32(ROWS, NCOL))(back, weights)
    new_weights, both_rows = call(join_kernel, (f32(2 * ROWS, NCOL), f32(2 * ROWS, RANK)))(
        half, swap(half), rows, swap(rows)
    )
    gram = call(
        gram_kernel, f32(RANK, RANK), in_specs=[vmem_spec(), any_spec()]
    )(subspace, both_rows)
    new_basis = call(refresh_kernel, f32(2 * ROWS, RANK))(gram, swap(gram), both_rows)
    return (new_weights, new_first, new_second, new_basis, new_gains, new_gain_first, new_gain_second)


def solution(mesh):
    in_specs = (
        P("rep", "grp", None),
        P("rep", None, "grp"),
        P("grp", None),
        P("grp", None),
        P("grp", None),
        P("grp", None),
        P(None, "grp"),
        P(None, "grp"),
        P(None, "grp"),
    )
    out_specs = (
        P("grp", None),
        P("grp", None),
        P("grp", None),
        P("grp", None),
        P(None, "grp"),
        P(None, "grp"),
        P(None, "grp"),
    )
    return jax.shard_map(body, mesh=mesh, in_specs=in_specs, out_specs=out_specs, check_vma=False)
```

```python
import functools

import jax
import jax.numpy as jnp
from jax import lax
from jax.experimental import pallas as pl
from jax.experimental.pallas import tpu as pltpu
from jax.sharding import PartitionSpec as P

NS_STEPS = 3

beta_first = 0.9
beta_second = 0.999
learn_rate = 0.1
galore_scale = 0.25
adam_eps = 1e-08

CHIPS = 64
ROWS = 8
NCOL = 9216
OWN = NCOL // CHIPS
RANK = 256
LANE = 128
PIECE = 16
BLOCK = 25
VMEM_LIMIT = 16 * 1024 * 1024

SWAP = [(0, 1), (1, 0)]


def dot(left, right, left_dim, right_dim):
    return lax.dot_general(
        left,
        right,
        (((left_dim,), (right_dim,)), ((), ())),
        precision=lax.Precision.HIGHEST,
        preferred_element_type=jnp.float32,
    )


def split(value):
    high = value.astype(jnp.bfloat16)
    return high, (value - high.astype(jnp.float32)).astype(jnp.bfloat16)


def split_dot(left, right, left_dim, right_dim):
    def one(a, b):
        return lax.dot_general(
            a, b, (((left_dim,), (right_dim,)), ((), ())), preferred_element_type=jnp.float32
        )

    return one(left[0], right[0]) + (one(left[0], right[1]) + one(left[1], right[0]))


def call(kernel, out_shape, scratch=(), **specs):
    return pl.pallas_call(
        kernel,
        out_shape=out_shape,
        **specs,
        scratch_shapes=list(scratch),
        compiler_params=pltpu.CompilerParams(vmem_limit_bytes=VMEM_LIMIT),
    )


def f32(*shape):
    return jax.ShapeDtypeStruct(shape, jnp.float32)


def any_spec():
    return pl.BlockSpec(memory_space=pl.ANY)


def vmem_spec():
    return pl.BlockSpec(memory_space=pltpu.VMEM)


def iota(axis):
    return lax.broadcasted_iota(jnp.int32, (ROWS, LANE), axis)


def half_rows(core):
    return pl.ds(pl.multiple_of(core * ROWS, ROWS), ROWS)


def swap_pieces(tile):
    row, piece = iota(0), iota(1) // PIECE
    for bit in (1, 2, 4):
        up = pltpu.roll(pltpu.roll(tile, ROWS - bit, 0), PIECE * bit, 1)
        down = pltpu.roll(pltpu.roll(tile, bit, 0), LANE - PIECE * bit, 1)
        row_set, piece_set = (row & bit) != 0, (piece & bit) != 0
        tile = jnp.where(row_set == piece_set, tile, jnp.where(piece_set, up, down))
    return tile


def octet(group):
    return pl.ds(BLOCK * 8 * group + BLOCK - 1, 8, stride=BLOCK)


def stage_kernel(grad_ref, basis_ref, gain_ref, grad_out, basis_out, gain_out):
    half = half_rows(lax.axis_index("rep"))
    grad_out[...] = grad_ref[half, :]
    basis_out[...] = basis_ref[half, :]
    gain_out[...] = jnp.zeros_like(gain_out)
    gain_out[:2, : 2 * ROWS] = gain_ref[...]


def pack_kernel(own_ref, other_ref, basis_ref, out_ref):
    half = half_rows(lax.axis_index("rep"))
    lane, piece = iota(1), iota(1) // PIECE
    low, high = basis_ref[:, :LANE], basis_ref[:, LANE:]
    for group in range(8):
        tiles = []
        for t in range(9):
            cols = pl.ds((9 * group + t) * LANE, LANE)
            tiles.append(own_ref[:, cols] + other_ref[half, cols])
        last = tiles[8]
        for j in range(8):
            at = BLOCK * (8 * group + j)
            out_ref[at : at + 8, :] = jnp.where(lane >= PIECE * j, tiles[j], tiles[j + 1])
            out_ref[at + 8 : at + 16, :] = low
            out_ref[at + 16 : at + 24, :] = high
            last = jnp.where(piece == j, tiles[j + 1], last)
        out_ref[octet(group), :] = swap_pieces(last)


def project_kernel(in_ref, grad_ref, basis_ref, out_ref, twice):
    piece = iota(1) // PIECE
    for group in range(8):
        last = swap_pieces(in_ref[octet(group), :])
        for j in range(8):
            chip = 8 * group + j
            at, rows = BLOCK * chip, slice(ROWS * chip, ROWS * chip + ROWS)
            grad_ref[rows, :LANE] = in_ref[at : at + 8, :]
            grad_ref[rows, LANE:] = jnp.where(piece == j, last, 0.0)
            basis_ref[rows, :LANE] = in_ref[at + 8 : at + 16, :]
            basis_ref[rows, LANE:] = in_ref[at + 16 : at + 24, :]
    product = dot(grad_ref[...], basis_ref[...], 0, 0)
    twice[:LANE, :] = product[:LANE]
    twice[LANE:, :] = product[:LANE]
    first = pl.multiple_of(lax.rem(lax.axis_index("grp"), 8) * PIECE, PIECE)
    out_ref[:LANE, :] = twice[pl.ds(first, LANE), :]
    out_ref[LANE:, :] = sum(
        product[LANE + PIECE * j : LANE + PIECE * (j + 1)] for j in range(8)
    )


def spread_columns(values, twice, out):
    twice[:LANE, :] = values[:LANE]
    twice[LANE:, :] = values[:LANE]
    first = pl.multiple_of(LANE - lax.rem(lax.axis_index("grp"), 8) * PIECE, PIECE)
    out[:LANE, :] = twice[pl.ds(first, LANE), :]
    for j in range(8):
        out[LANE + PIECE * j : LANE + PIECE * (j + 1), :] = values[LANE:]


def adam(value, first, second):
    corr_first = 1.0 - beta_first**10
    corr_second = 1.0 - beta_second**10
    new_first = beta_first * first + (1.0 - beta_first) * value
    new_second = beta_second * second + (1.0 - beta_second) * value * value
    direction = new_first / corr_first / (jnp.sqrt(new_second / corr_second) + adam_eps)
    return new_first, new_second, direction


def subspace_update_kernel(
    grad_ref, basis_ref, own_ref, other_ref, first_ref, second_ref,
    out_ref, twice, projected_wide, direction_wide,
):
    projected = own_ref[...] + other_ref[...]
    _, _, direction = adam(projected, first_ref[...], second_ref[...])
    spread_columns(projected, twice, projected_wide)
    spread_columns(direction, twice, direction_wide)
    subspace = split_dot(split(grad_ref[...]), split(projected_wide[...]), 1, 0)
    update = split_dot(split(basis_ref[...]), split(direction_wide[...]), 1, 1)
    diagonal = iota(0) == iota(1) // PIECE
    for chip in range(CHIPS):
        at, rows = BLOCK * chip, slice(ROWS * chip, ROWS * chip + ROWS)
        out_ref[at : at + 8, :] = update[rows, :LANE]
        out_ref[at + 8 : at + 16, :] = subspace[rows, :LANE]
        out_ref[at + 16 : at + 24, :] = subspace[rows, LANE:]
        out_ref[at + 24 : at + 25, :] = jnp.sum(
            jnp.where(diagonal, update[rows, LANE:], 0.0), axis=0, keepdims=True
        )


def subspace_kernel(in_ref, gain_ref, rows_ref, out_ref):
    low = sum(in_ref[BLOCK * chip + 8 : BLOCK * chip + 16, :] for chip in range(CHIPS))
    high = sum(in_ref[BLOCK * chip + 16 : BLOCK * chip + 24, :] for chip in range(CHIPS))
    rows = jnp.concatenate([low, high], axis=1)
    rows_ref[:ROWS, :] = rows
    rows_ref[ROWS:, :LANE] = gain_ref[...]
    rows_ref[ROWS:, LANE:] = jnp.zeros((ROWS, LANE), jnp.float32)
    out_ref[...] = jnp.broadcast_to(rows[None], out_ref.shape)


def weights_kernel(
    in_ref, weights_ref, own_ref, other_ref, first_ref, second_ref,
    out_ref, new_first_ref, new_second_ref,
):
    projected = own_ref[...] + other_ref[...]
    new_first_ref[...], new_second_ref[...], _ = adam(projected, first_ref[...], second_ref[...])
    half = half_rows(lax.axis_index("rep"))
    lane = iota(1)
    for group in range(8):
        last = swap_pieces(in_ref[octet(group), :])
        mains = [
            in_ref[BLOCK * (8 * group + j) : BLOCK * (8 * group + j) + 8, :] for j in range(8)
        ]
        for t in range(9):
            update = last
            if t < 8:
                update = jnp.where(lane >= PIECE * t, mains[t], update)
            if t > 0:
                update = jnp.where(lane < PIECE * (t - 1), mains[t - 1], update)
            cols = pl.ds((9 * group + t) * LANE, LANE)
            out_ref[:, cols] = weights_ref[half, cols] - learn_rate * galore_scale * update


def join_kernel(
    own_ref, other_ref, rows_ref, other_rows_ref, gains_ref, gain_first_ref, gain_second_ref,
    out_ref, rows_out, new_gains_ref, new_gain_first_ref, new_gain_second_ref,
):
    core = lax.axis_index("rep")
    out_ref[half_rows(core), :] = own_ref[...]
    out_ref[half_rows(1 - core), :] = other_ref[...]
    rows_out[half_rows(core), :] = rows_ref[:ROWS, :]
    rows_out[half_rows(1 - core), :] = other_rows_ref[:ROWS, :]
    gain = (rows_ref[ROWS:, :] + other_rows_ref[ROWS:, :])[:2, : 2 * ROWS]
    new_first, new_second, direction = adam(gain, gain_first_ref[...], gain_second_ref[...])
    new_gain_first_ref[...] = new_first
    new_gain_second_ref[...] = new_second
    new_gains_ref[...] = gains_ref[...] - learn_rate * direction


def gram_kernel(in_ref, rows_ref, out_ref):
    subspace = split(in_ref[...])
    out_ref[...] = split_dot(subspace, subspace, 0, 0)


def refresh_kernel(own_gram_ref, other_gram_ref, rows_ref, out_ref):
    gram = own_gram_ref[...] + other_gram_ref[...]
    scale = jnp.sqrt(jnp.sqrt(jnp.sum(gram * gram, keepdims=True) + 1e-06))
    iterate = rows_ref[...] / scale
    current = gram / scale / scale
    diagonal = lax.broadcasted_iota(jnp.int32, (RANK, RANK), 0) == lax.broadcasted_iota(
        jnp.int32, (RANK, RANK), 1
    )
    for step in range(NS_STEPS):
        factor = split(jnp.where(diagonal, 1.5, 0.0) - 0.5 * current)
        iterate = split_dot(split(iterate), factor, 1, 0)
        if step + 1 < NS_STEPS:
            current = split_dot(split(split_dot(factor, split(current), 1, 0)), factor, 1, 0)
    out_ref[...] = iterate


def body(
    grad_parts,
    gain_grad_parts,
    weights,
    basis,
    moment_first,
    moment_second,
    gains,
    gain_first,
    gain_second,
):
    swap = functools.partial(lax.ppermute, axis_name="rep", perm=SWAP)
    vmem = pltpu.VMEM

    def exchange(blocks):
        out = lax.all_to_all(blocks, "grp", split_axis=0, concat_axis=0, tiled=True)
        return out

    def exchange_blocks(blocks):
        return exchange(blocks.reshape(CHIPS * BLOCK, 1, LANE)).reshape(CHIPS * BLOCK, LANE)

    wide = f32(CHIPS * ROWS, RANK)
    small = f32(2, 2 * ROWS)
    local_grad = grad_parts[0]
    other_grad = swap(local_grad)
    own_grad, own_basis, gain = call(
        stage_kernel, (f32(ROWS, NCOL), f32(ROWS, RANK), f32(ROWS, LANE))
    )(local_grad, basis, gain_grad_parts[0])
    packed = call(pack_kernel, f32(CHIPS * BLOCK, LANE))(own_grad, other_grad, own_basis)
    columns, full_basis, part = call(
        project_kernel, (wide, wide, f32(OWN, RANK)), [vmem((2 * LANE, RANK), jnp.float32)]
    )(exchange_blocks(packed))
    other_part = swap(part)
    out = call(
        subspace_update_kernel,
        f32(CHIPS * BLOCK, LANE),
        [vmem((2 * LANE, RANK), jnp.float32)] * 3,
    )(columns, full_basis, part, other_part, moment_first, moment_second)
    back = exchange_blocks(out)
    rows, spread = call(subspace_kernel, (f32(2 * ROWS, RANK), f32(CHIPS, ROWS, RANK)))(back, gain)
    subspace = exchange(spread).reshape(CHIPS * ROWS, RANK)
    half, new_first, new_second = call(
        weights_kernel, (f32(ROWS, NCOL), f32(OWN, RANK), f32(OWN, RANK))
    )(back, weights, part, other_part, moment_first, moment_second)
    new_weights, both_rows, new_gains, new_gain_first, new_gain_second = call(
        join_kernel, (f32(2 * ROWS, NCOL), f32(2 * ROWS, RANK), small, small, small)
    )(half, swap(half), rows, swap(rows), gains, gain_first, gain_second)
    gram = call(
        gram_kernel, f32(RANK, RANK), in_specs=[vmem_spec(), any_spec()]
    )(subspace, both_rows)
    new_basis = call(refresh_kernel, f32(2 * ROWS, RANK))(gram, swap(gram), both_rows)
    return (new_weights, new_first, new_second, new_basis, new_gains, new_gain_first, new_gain_second)


def solution(mesh):
    in_specs = (
        P("rep", "grp", None),
        P("rep", None, "grp"),
        P("grp", None),
        P("grp", None),
        P("grp", None),
        P("grp", None),
        P(None, "grp"),
        P(None, "grp"),
        P(None, "grp"),
    )
    out_specs = (
        P("grp", None),
        P("grp", None),
        P("grp", None),
        P("grp", None),
        P(None, "grp"),
        P(None, "grp"),
        P(None, "grp"),
    )
    return jax.shard_map(body, mesh=mesh, in_specs=in_specs, out_specs=out_specs, check_vma=False)
```

```python
import functools

import jax
import jax.numpy as jnp
from jax import lax
from jax.experimental import pallas as pl
from jax.experimental.pallas import tpu as pltpu
from jax.sharding import PartitionSpec as P

beta_first = 0.9
beta_second = 0.999
learn_rate = 0.1
galore_scale = 0.25
adam_eps = 1e-08

CHIPS = 64
ROWS = 8
NCOL = 9216
OWN = NCOL // CHIPS
RANK = 256
LANE = 128
PIECE = 16
BLOCK = 25
VMEM_LIMIT = 16 * 1024 * 1024

SWAP = [(0, 1), (1, 0)]


def dot(left, right, left_dim, right_dim):
    return lax.dot_general(
        left,
        right,
        (((left_dim,), (right_dim,)), ((), ())),
        precision=lax.Precision.HIGHEST,
        preferred_element_type=jnp.float32,
    )


def split(value):
    high = value.astype(jnp.bfloat16)
    return high, (value - high.astype(jnp.float32)).astype(jnp.bfloat16)


def split_dot(left, right, left_dim, right_dim):
    def one(a, b):
        return lax.dot_general(
            a, b, (((left_dim,), (right_dim,)), ((), ())), preferred_element_type=jnp.float32
        )

    return one(left[0], right[0]) + (one(left[0], right[1]) + one(left[1], right[0]))


def call(kernel, out_shape, scratch=(), **specs):
    return pl.pallas_call(
        kernel,
        out_shape=out_shape,
        **specs,
        scratch_shapes=list(scratch),
        compiler_params=pltpu.CompilerParams(vmem_limit_bytes=VMEM_LIMIT),
    )


def f32(*shape):
    return jax.ShapeDtypeStruct(shape, jnp.float32)


def any_spec():
    return pl.BlockSpec(memory_space=pl.ANY)


def vmem_spec():
    return pl.BlockSpec(memory_space=pltpu.VMEM)


def iota(axis):
    return lax.broadcasted_iota(jnp.int32, (ROWS, LANE), axis)


def half_rows(core):
    return pl.ds(pl.multiple_of(core * ROWS, ROWS), ROWS)


def swap_pieces(tile):
    row, piece = iota(0), iota(1) // PIECE
    for bit in (1, 2, 4):
        up = pltpu.roll(pltpu.roll(tile, ROWS - bit, 0), PIECE * bit, 1)
        down = pltpu.roll(pltpu.roll(tile, bit, 0), LANE - PIECE * bit, 1)
        row_set, piece_set = (row & bit) != 0, (piece & bit) != 0
        tile = jnp.where(row_set == piece_set, tile, jnp.where(piece_set, up, down))
    return tile


def octet(group):
    return pl.ds(BLOCK * 8 * group + BLOCK - 1, 8, stride=BLOCK)


def stage_kernel(grad_ref, basis_ref, gain_ref, grad_out, basis_out, gain_out, gain, sems):
    half = half_rows(lax.axis_index("rep"))
    copies = [
        pltpu.make_async_copy(grad_ref.at[half, :], grad_out, sems.at[0]),
        pltpu.make_async_copy(basis_ref.at[half, :], basis_out, sems.at[1]),
        pltpu.make_async_copy(gain_ref, gain, sems.at[2]),
    ]
    for copy in copies:
        copy.start()
    gain_out[...] = jnp.zeros_like(gain_out)
    for copy in copies:
        copy.wait()
    gain_out[:2, : 2 * ROWS] = gain[...]


def pack_kernel(own_ref, other_ref, basis_ref, out_ref):
    half = half_rows(lax.axis_index("rep"))
    lane, piece = iota(1), iota(1) // PIECE
    low, high = basis_ref[:, :LANE], basis_ref[:, LANE:]
    for group in range(8):
        tiles = []
        for t in range(9):
            cols = pl.ds((9 * group + t) * LANE, LANE)
            tiles.append(own_ref[:, cols] + other_ref[half, cols])
        last = tiles[8]
        for j in range(8):
            at = BLOCK * (8 * group + j)
            out_ref[at : at + 8, :] = jnp.where(lane >= PIECE * j, tiles[j], tiles[j + 1])
            out_ref[at + 8 : at + 16, :] = low
            out_ref[at + 16 : at + 24, :] = high
            last = jnp.where(piece == j, tiles[j + 1], last)
        out_ref[octet(group), :] = swap_pieces(last)


def project_kernel(in_ref, grad_ref, basis_ref, out_ref, twice):
    piece = iota(1) // PIECE
    for group in range(8):
        last = swap_pieces(in_ref[octet(group), :])
        for j in range(8):
            chip = 8 * group + j
            at, rows = BLOCK * chip, slice(ROWS * chip, ROWS * chip + ROWS)
            grad_ref[rows, :LANE] = in_ref[at : at + 8, :]
            grad_ref[rows, LANE:] = jnp.where(piece == j, last, 0.0)
            basis_ref[rows, :LANE] = in_ref[at + 8 : at + 16, :]
            basis_ref[rows, LANE:] = in_ref[at + 16 : at + 24, :]
    product = dot(grad_ref[...], basis_ref[...], 0, 0)
    twice[:LANE, :] = product[:LANE]
    twice[LANE:, :] = product[:LANE]
    first = pl.multiple_of(lax.rem(lax.axis_index("grp"), 8) * PIECE, PIECE)
    out_ref[:LANE, :] = twice[pl.ds(first, LANE), :]
    out_ref[LANE:, :] = sum(
        product[LANE + PIECE * j : LANE + PIECE * (j + 1)] for j in range(8)
    )


def spread_columns(values, twice, out):
    twice[:LANE, :] = values[:LANE]
    twice[LANE:, :] = values[:LANE]
    first = pl.multiple_of(LANE - lax.rem(lax.axis_index("grp"), 8) * PIECE, PIECE)
    out[:LANE, :] = twice[pl.ds(first, LANE), :]
    for j in range(8):
        out[LANE + PIECE * j : LANE + PIECE * (j + 1), :] = values[LANE:]


def adam(value, first, second):
    corr_first = 1.0 - beta_first**10
    corr_second = 1.0 - beta_second**10
    new_first = beta_first * first + (1.0 - beta_first) * value
    new_second = beta_second * second + (1.0 - beta_second) * value * value
    direction = new_first / corr_first / (jnp.sqrt(new_second / corr_second) + adam_eps)
    return new_first, new_second, direction


def subspace_update_kernel(
    grad_ref, basis_ref, own_ref, other_ref, first_ref, second_ref,
    out_ref, twice, projected_wide, direction_wide,
):
    projected = own_ref[...] + other_ref[...]
    _, _, direction = adam(projected, first_ref[...], second_ref[...])
    spread_columns(projected, twice, projected_wide)
    spread_columns(direction, twice, direction_wide)
    subspace = split_dot(split(grad_ref[...]), split(projected_wide[...]), 1, 0)
    update = split_dot(split(basis_ref[...]), split(direction_wide[...]), 1, 1)
    diagonal = iota(0) == iota(1) // PIECE
    for chip in range(CHIPS):
        at, rows = BLOCK * chip, slice(ROWS * chip, ROWS * chip + ROWS)
        out_ref[at : at + 8, :] = update[rows, :LANE]
        out_ref[at + 8 : at + 16, :] = subspace[rows, :LANE]
        out_ref[at + 16 : at + 24, :] = subspace[rows, LANE:]
        out_ref[at + 24 : at + 25, :] = jnp.sum(
            jnp.where(diagonal, update[rows, LANE:], 0.0), axis=0, keepdims=True
        )


def subspace_kernel(in_ref, gain_ref, rows_ref, out_ref):
    low = sum(in_ref[BLOCK * chip + 8 : BLOCK * chip + 16, :] for chip in range(CHIPS))
    high = sum(in_ref[BLOCK * chip + 16 : BLOCK * chip + 24, :] for chip in range(CHIPS))
    rows = jnp.concatenate([low, high], axis=1)
    rows_ref[:ROWS, :] = rows
    rows_ref[ROWS:, :LANE] = gain_ref[...]
    rows_ref[ROWS:, LANE:] = jnp.zeros((ROWS, LANE), jnp.float32)
    out_ref[...] = jnp.broadcast_to(rows[None], out_ref.shape)


def weights_kernel(
    in_ref, weights_ref, own_ref, other_ref, first_ref, second_ref,
    out_ref, new_first_ref, new_second_ref,
):
    projected = own_ref[...] + other_ref[...]
    new_first_ref[...], new_second_ref[...], _ = adam(projected, first_ref[...], second_ref[...])
    half = half_rows(lax.axis_index("rep"))
    lane = iota(1)
    for group in range(8):
        last = swap_pieces(in_ref[octet(group), :])
        mains = [
            in_ref[BLOCK * (8 * group + j) : BLOCK * (8 * group + j) + 8, :] for j in range(8)
        ]
        for t in range(9):
            update = last
            if t < 8:
                update = jnp.where(lane >= PIECE * t, mains[t], update)
            if t > 0:
                update = jnp.where(lane < PIECE * (t - 1), mains[t - 1], update)
            cols = pl.ds((9 * group + t) * LANE, LANE)
            out_ref[:, cols] = weights_ref[half, cols] - learn_rate * galore_scale * update


def join_kernel(
    own_ref, other_ref, rows_ref, other_rows_ref, gains_ref, gain_first_ref, gain_second_ref,
    out_ref, rows_out, new_gains_ref, new_gain_first_ref, new_gain_second_ref,
):
    core = lax.axis_index("rep")
    out_ref[half_rows(core), :] = own_ref[...]
    out_ref[half_rows(1 - core), :] = other_ref[...]
    rows_out[half_rows(core), :] = rows_ref[:ROWS, :]
    rows_out[half_rows(1 - core), :] = other_rows_ref[:ROWS, :]
    gain = (rows_ref[ROWS:, :] + other_rows_ref[ROWS:, :])[:2, : 2 * ROWS]
    new_first, new_second, direction = adam(gain, gain_first_ref[...], gain_second_ref[...])
    new_gain_first_ref[...] = new_first
    new_gain_second_ref[...] = new_second
    new_gains_ref[...] = gains_ref[...] - learn_rate * direction


def gram_kernel(in_ref, rows_ref, out_ref):
    subspace = split(in_ref[...])
    out_ref[...] = split_dot(subspace, subspace, 0, 0)


def refresh_kernel(own_gram_ref, other_gram_ref, rows_ref, out_ref):
    diagonal = lax.broadcasted_iota(jnp.int32, (RANK, RANK), 0) == lax.broadcasted_iota(
        jnp.int32, (RANK, RANK), 1
    )

    def shifted(amount, value):
        return jnp.where(diagonal, amount, 0.0) + value

    gram = own_gram_ref[...] + other_gram_ref[...]
    gram_split = split(gram)
    gram_square = split_dot(gram_split, gram_split, 1, 0)
    scale = jnp.sqrt(jnp.sqrt(jnp.sum(gram * gram, keepdims=True) + 1e-06))
    current = gram / scale / scale
    square = gram_square / scale / scale / scale / scale
    iterate = split_dot(split(rows_ref[...] / scale), split(shifted(1.5, -0.5 * current)), 1, 0)
    current = split_dot(
        split(current), split(shifted(2.25, 0.25 * square - 1.5 * current)), 1, 0
    )
    current_split = split(current)
    square = split_dot(current_split, current_split, 1, 0)
    iterate = split_dot(split(iterate), split(shifted(1.5, -0.5 * current)), 1, 0)
    last = split_dot(split(iterate), current_split, 1, 0)
    last = split_dot(split(last), split(shifted(2.25, 0.25 * square - 1.5 * current)), 1, 0)
    out_ref[...] = 1.5 * iterate - 0.5 * last


def body(
    grad_parts,
    gain_grad_parts,
    weights,
    basis,
    moment_first,
    moment_second,
    gains,
    gain_first,
    gain_second,
):
    swap = functools.partial(lax.ppermute, axis_name="rep", perm=SWAP)
    vmem = pltpu.VMEM
    hbm = functools.partial(pltpu.with_memory_space_constraint, memory_space=pltpu.HBM)

    def exchange(blocks):
        out = lax.all_to_all(blocks, "grp", split_axis=0, concat_axis=0, tiled=True)
        return out

    def exchange_blocks(blocks):
        return exchange(blocks.reshape(CHIPS * BLOCK, 1, LANE)).reshape(CHIPS * BLOCK, LANE)

    wide = f32(CHIPS * ROWS, RANK)
    small = f32(2, 2 * ROWS)
    local_grad = grad_parts[0]
    other_grad = swap(local_grad)
    own_grad, own_basis, gain = call(
        stage_kernel,
        (f32(ROWS, NCOL), f32(ROWS, RANK), f32(ROWS, LANE)),
        [vmem((2, 2 * ROWS), jnp.float32), pltpu.SemaphoreType.DMA((3,))],
        in_specs=[pl.BlockSpec(memory_space=pltpu.HBM)] * 3,
    )(*(hbm(x) for x in (local_grad, basis, gain_grad_parts[0])))
    packed = call(pack_kernel, f32(CHIPS * BLOCK, LANE))(own_grad, other_grad, own_basis)
    columns, full_basis, part = call(
        project_kernel, (wide, wide, f32(OWN, RANK)), [vmem((2 * LANE, RANK), jnp.float32)]
    )(exchange_blocks(packed))
    other_part = swap(part)
    out = call(
        subspace_update_kernel,
        f32(CHIPS * BLOCK, LANE),
        [vmem((2 * LANE, RANK), jnp.float32)] * 3,
    )(columns, full_basis, part, other_part, moment_first, moment_second)
    back = exchange_blocks(out)
    rows, spread = call(
        subspace_kernel, (f32(2 * ROWS, RANK), vmem((CHIPS, ROWS, RANK), jnp.float32))
    )(back, gain)
    subspace = exchange(spread).reshape(CHIPS * ROWS, RANK)
    half, new_first, new_second = call(
        weights_kernel, (f32(ROWS, NCOL), f32(OWN, RANK), f32(OWN, RANK))
    )(back, weights, part, other_part, moment_first, moment_second)
    new_weights, both_rows, new_gains, new_gain_first, new_gain_second = call(
        join_kernel, (f32(2 * ROWS, NCOL), f32(2 * ROWS, RANK), small, small, small)
    )(half, swap(half), rows, swap(rows), gains, gain_first, gain_second)
    gram = call(
        gram_kernel, f32(RANK, RANK), in_specs=[vmem_spec(), any_spec()]
    )(subspace, both_rows)
    new_basis = call(refresh_kernel, f32(2 * ROWS, RANK))(gram, swap(gram), both_rows)
    return (new_weights, new_first, new_second, new_basis, new_gains, new_gain_first, new_gain_second)


def solution(mesh):
    in_specs = (
        P("rep", "grp", None),
        P("rep", None, "grp"),
        P("grp", None),
        P("grp", None),
        P("grp", None),
        P("grp", None),
        P(None, "grp"),
        P(None, "grp"),
        P(None, "grp"),
    )
    out_specs = (
        P("grp", None),
        P("grp", None),
        P("grp", None),
        P("grp", None),
        P(None, "grp"),
        P(None, "grp"),
        P(None, "grp"),
    )
    return jax.shard_map(body, mesh=mesh, in_specs=in_specs, out_specs=out_specs, check_vma=False)
```

```python
import functools

import jax
import jax.numpy as jnp
from jax import lax
from jax.experimental import pallas as pl
from jax.experimental.pallas import tpu as pltpu
from jax.sharding import PartitionSpec as P

beta_first = 0.9
beta_second = 0.999
learn_rate = 0.1
galore_scale = 0.25
adam_eps = 1e-08

CHIPS = 64
ROWS = 8
NCOL = 9216
OWN = NCOL // CHIPS
RANK = 256
LANE = 128
PIECE = 16
BLOCK = 25
VMEM_LIMIT = 16 * 1024 * 1024

SWAP = [(0, 1), (1, 0)]


def dot(left, right, left_dim, right_dim):
    return lax.dot_general(
        left,
        right,
        (((left_dim,), (right_dim,)), ((), ())),
        precision=lax.Precision.HIGHEST,
        preferred_element_type=jnp.float32,
    )


def split(value):
    high = value.astype(jnp.bfloat16)
    return high, (value - high.astype(jnp.float32)).astype(jnp.bfloat16)


def split_dot(left, right, left_dim, right_dim):
    def one(a, b):
        return lax.dot_general(
            a, b, (((left_dim,), (right_dim,)), ((), ())), preferred_element_type=jnp.float32
        )

    return one(left[0], right[0]) + (one(left[0], right[1]) + one(left[1], right[0]))


def call(kernel, out_shape, scratch=(), **specs):
    return pl.pallas_call(
        kernel,
        out_shape=out_shape,
        **specs,
        scratch_shapes=list(scratch),
        compiler_params=pltpu.CompilerParams(vmem_limit_bytes=VMEM_LIMIT),
    )


def f32(*shape):
    return jax.ShapeDtypeStruct(shape, jnp.float32)


def any_spec():
    return pl.BlockSpec(memory_space=pl.ANY)


def vmem_spec():
    return pl.BlockSpec(memory_space=pltpu.VMEM)


def iota(axis):
    return lax.broadcasted_iota(jnp.int32, (ROWS, LANE), axis)


def half_rows(core):
    return pl.ds(pl.multiple_of(core * ROWS, ROWS), ROWS)


def swap_pieces(tile):
    row, piece = iota(0), iota(1) // PIECE
    for bit in (1, 2, 4):
        up = pltpu.roll(pltpu.roll(tile, ROWS - bit, 0), PIECE * bit, 1)
        down = pltpu.roll(pltpu.roll(tile, bit, 0), LANE - PIECE * bit, 1)
        row_set, piece_set = (row & bit) != 0, (piece & bit) != 0
        tile = jnp.where(row_set == piece_set, tile, jnp.where(piece_set, up, down))
    return tile


def octet(group):
    return pl.ds(BLOCK * 8 * group + BLOCK - 1, 8, stride=BLOCK)


def stage_kernel(grad_ref, basis_ref, gain_ref, grad_out, basis_out, gain_out, gain, sems):
    half = half_rows(lax.axis_index("rep"))
    copies = [
        pltpu.make_async_copy(grad_ref.at[half, :], grad_out, sems.at[0]),
        pltpu.make_async_copy(basis_ref.at[half, :], basis_out, sems.at[1]),
        pltpu.make_async_copy(gain_ref, gain, sems.at[2]),
    ]
    for copy in copies:
        copy.start()
    gain_out[...] = jnp.zeros_like(gain_out)
    for copy in copies:
        copy.wait()
    gain_out[:2, : 2 * ROWS] = gain[...]


def pack_kernel(own_ref, other_ref, basis_ref, out_ref):
    half = half_rows(lax.axis_index("rep"))
    lane, piece = iota(1), iota(1) // PIECE
    low, high = basis_ref[:, :LANE], basis_ref[:, LANE:]
    for group in range(8):
        tiles = []
        for t in range(9):
            cols = pl.ds((9 * group + t) * LANE, LANE)
            tiles.append(own_ref[:, cols] + other_ref[half, cols])
        last = tiles[8]
        for j in range(8):
            at = BLOCK * (8 * group + j)
            out_ref[at : at + 8, :] = jnp.where(lane >= PIECE * j, tiles[j], tiles[j + 1])
            out_ref[at + 8 : at + 16, :] = low
            out_ref[at + 16 : at + 24, :] = high
            last = jnp.where(piece == j, tiles[j + 1], last)
        out_ref[octet(group), :] = swap_pieces(last)


def project_kernel(in_ref, grad_ref, basis_ref, out_ref, twice):
    piece = iota(1) // PIECE
    for group in range(8):
        last = swap_pieces(in_ref[octet(group), :])
        for j in range(8):
            chip = 8 * group + j
            at, rows = BLOCK * chip, slice(ROWS * chip, ROWS * chip + ROWS)
            grad_ref[rows, :LANE] = in_ref[at : at + 8, :]
            grad_ref[rows, LANE:] = jnp.where(piece == j, last, 0.0)
            basis_ref[rows, :LANE] = in_ref[at + 8 : at + 16, :]
            basis_ref[rows, LANE:] = in_ref[at + 16 : at + 24, :]
    product = dot(grad_ref[...], basis_ref[...], 0, 0)
    twice[:LANE, :] = product[:LANE]
    twice[LANE:, :] = product[:LANE]
    first = pl.multiple_of(lax.rem(lax.axis_index("grp"), 8) * PIECE, PIECE)
    out_ref[:LANE, :] = twice[pl.ds(first, LANE), :]
    out_ref[LANE:, :] = sum(
        product[LANE + PIECE * j : LANE + PIECE * (j + 1)] for j in range(8)
    )


def spread_columns(values, twice, out):
    twice[:LANE, :] = values[:LANE]
    twice[LANE:, :] = values[:LANE]
    first = pl.multiple_of(LANE - lax.rem(lax.axis_index("grp"), 8) * PIECE, PIECE)
    out[:LANE, :] = twice[pl.ds(first, LANE), :]
    for j in range(8):
        out[LANE + PIECE * j : LANE + PIECE * (j + 1), :] = values[LANE:]


def adam(value, first, second):
    corr_first = 1.0 - beta_first**10
    corr_second = 1.0 - beta_second**10
    new_first = beta_first * first + (1.0 - beta_first) * value
    new_second = beta_second * second + (1.0 - beta_second) * value * value
    direction = new_first / corr_first / (jnp.sqrt(new_second / corr_second) + adam_eps)
    return new_first, new_second, direction


def subspace_update_kernel(
    grad_ref, basis_ref, own_ref, other_ref, first_ref, second_ref,
    out_ref, twice, projected_wide, direction_wide,
):
    projected = own_ref[...] + other_ref[...]
    _, _, direction = adam(projected, first_ref[...], second_ref[...])
    spread_columns(projected, twice, projected_wide)
    spread_columns(direction, twice, direction_wide)
    subspace = split_dot(split(grad_ref[...]), split(projected_wide[...]), 1, 0)
    update = split_dot(split(basis_ref[...]), split(direction_wide[...]), 1, 1)
    diagonal = iota(0) == iota(1) // PIECE
    for chip in range(CHIPS):
        at, rows = BLOCK * chip, slice(ROWS * chip, ROWS * chip + ROWS)
        out_ref[at : at + 8, :] = update[rows, :LANE]
        out_ref[at + 8 : at + 16, :] = subspace[rows, :LANE]
        out_ref[at + 16 : at + 24, :] = subspace[rows, LANE:]
        out_ref[at + 24 : at + 25, :] = jnp.sum(
            jnp.where(diagonal, update[rows, LANE:], 0.0), axis=0, keepdims=True
        )


def subspace_kernel(in_ref, gain_ref, rows_ref, out_ref):
    low = sum(in_ref[BLOCK * chip + 8 : BLOCK * chip + 16, :] for chip in range(CHIPS))
    high = sum(in_ref[BLOCK * chip + 16 : BLOCK * chip + 24, :] for chip in range(CHIPS))
    rows = jnp.concatenate([low, high], axis=1)
    rows_ref[:ROWS, :] = rows
    rows_ref[ROWS:, :LANE] = gain_ref[...]
    rows_ref[ROWS:, LANE:] = jnp.zeros((ROWS, LANE), jnp.float32)
    out_ref[...] = jnp.broadcast_to(rows[None], out_ref.shape)


def weights_kernel(
    in_ref, weights_ref, own_ref, other_ref, first_ref, second_ref,
    out_ref, new_first_ref, new_second_ref,
):
    projected = own_ref[...] + other_ref[...]
    new_first_ref[...], new_second_ref[...], _ = adam(projected, first_ref[...], second_ref[...])
    half = half_rows(lax.axis_index("rep"))
    lane = iota(1)
    for group in range(8):
        last = swap_pieces(in_ref[octet(group), :])
        mains = [
            in_ref[BLOCK * (8 * group + j) : BLOCK * (8 * group + j) + 8, :] for j in range(8)
        ]
        for t in range(9):
            update = last
            if t < 8:
                update = jnp.where(lane >= PIECE * t, mains[t], update)
            if t > 0:
                update = jnp.where(lane < PIECE * (t - 1), mains[t - 1], update)
            cols = pl.ds((9 * group + t) * LANE, LANE)
            out_ref[:, cols] = weights_ref[half, cols] - learn_rate * galore_scale * update


def join_kernel(
    own_ref, other_ref, rows_ref, other_rows_ref, gains_ref, gain_first_ref, gain_second_ref,
    out_ref, rows_out, new_gains_ref, new_gain_first_ref, new_gain_second_ref,
):
    core = lax.axis_index("rep")
    out_ref[half_rows(core), :] = own_ref[...]
    out_ref[half_rows(1 - core), :] = other_ref[...]
    rows_out[half_rows(core), :] = rows_ref[:ROWS, :]
    rows_out[half_rows(1 - core), :] = other_rows_ref[:ROWS, :]
    gain = (rows_ref[ROWS:, :] + other_rows_ref[ROWS:, :])[:2, : 2 * ROWS]
    new_first, new_second, direction = adam(gain, gain_first_ref[...], gain_second_ref[...])
    new_gain_first_ref[...] = new_first
    new_gain_second_ref[...] = new_second
    new_gains_ref[...] = gains_ref[...] - learn_rate * direction


def gram_kernel(in_ref, rows_ref, out_ref):
    subspace = split(in_ref[...])
    out_ref[...] = split_dot(subspace, subspace, 0, 0)


def refresh_kernel(own_gram_ref, other_gram_ref, rows_ref, out_ref):
    gram = own_gram_ref[...] + other_gram_ref[...]
    gram_split = split(gram)
    gram_square = split_dot(gram_split, gram_split, 1, 0)
    scale = jnp.sqrt(jnp.sqrt(jnp.sum(gram * gram, keepdims=True) + 1e-06))
    inverse = 1.0 / (scale * scale)
    current = gram * inverse
    square = jnp.where(scale < jnp.inf, gram_square, 0.0) * inverse * inverse
    current_split = split(current)
    iterate = rows_ref[...] / scale
    iterate = 1.5 * iterate - 0.5 * split_dot(split(iterate), current_split, 1, 0)
    current = 2.25 * current + split_dot(
        current_split, split(0.25 * square - 1.5 * current), 1, 0
    )
    current_split = split(current)
    square = split_dot(current_split, current_split, 1, 0)
    iterate = 1.5 * iterate - 0.5 * split_dot(split(iterate), current_split, 1, 0)
    last = split_dot(split(iterate), current_split, 1, 0)
    last = 2.25 * last + split_dot(split(last), split(0.25 * square - 1.5 * current), 1, 0)
    out_ref[...] = 1.5 * iterate - 0.5 * last


def body(
    grad_parts,
    gain_grad_parts,
    weights,
    basis,
    moment_first,
    moment_second,
    gains,
    gain_first,
    gain_second,
):
    swap = functools.partial(lax.ppermute, axis_name="rep", perm=SWAP)
    vmem = pltpu.VMEM
    hbm = functools.partial(pltpu.with_memory_space_constraint, memory_space=pltpu.HBM)

    def exchange(blocks):
        out = lax.all_to_all(blocks, "grp", split_axis=0, concat_axis=0, tiled=True)
        return out

    def exchange_blocks(blocks):
        return exchange(blocks.reshape(CHIPS * BLOCK, 1, LANE)).reshape(CHIPS * BLOCK, LANE)

    wide = f32(CHIPS * ROWS, RANK)
    small = f32(2, 2 * ROWS)
    local_grad = grad_parts[0]
    other_grad = swap(local_grad)
    own_grad, own_basis, gain = call(
        stage_kernel,
        (f32(ROWS, NCOL), f32(ROWS, RANK), f32(ROWS, LANE)),
        [vmem((2, 2 * ROWS), jnp.float32), pltpu.SemaphoreType.DMA((3,))],
        in_specs=[pl.BlockSpec(memory_space=pltpu.HBM)] * 3,
    )(*(hbm(x) for x in (local_grad, basis, gain_grad_parts[0])))
    packed = call(pack_kernel, f32(CHIPS * BLOCK, LANE))(own_grad, other_grad, own_basis)
    columns, full_basis, part = call(
        project_kernel, (wide, wide, f32(OWN, RANK)), [vmem((2 * LANE, RANK), jnp.float32)]
    )(exchange_blocks(packed))
    other_part = swap(part)
    out = call(
        subspace_update_kernel,
        f32(CHIPS * BLOCK, LANE),
        [vmem((2 * LANE, RANK), jnp.float32)] * 3,
    )(columns, full_basis, part, other_part, moment_first, moment_second)
    back = exchange_blocks(out)
    rows, spread = call(
        subspace_kernel, (f32(2 * ROWS, RANK), vmem((CHIPS, ROWS, RANK), jnp.float32))
    )(back, gain)
    subspace = exchange(spread).reshape(CHIPS * ROWS, RANK)
    half, new_first, new_second = call(
        weights_kernel, (f32(ROWS, NCOL), f32(OWN, RANK), f32(OWN, RANK))
    )(back, weights, part, other_part, moment_first, moment_second)
    new_weights, both_rows, new_gains, new_gain_first, new_gain_second = call(
        join_kernel, (f32(2 * ROWS, NCOL), f32(2 * ROWS, RANK), small, small, small)
    )(half, swap(half), rows, swap(rows), gains, gain_first, gain_second)
    gram = call(
        gram_kernel, f32(RANK, RANK), in_specs=[vmem_spec(), any_spec()]
    )(subspace, both_rows)
    new_basis = call(refresh_kernel, f32(2 * ROWS, RANK))(gram, swap(gram), both_rows)
    return (new_weights, new_first, new_second, new_basis, new_gains, new_gain_first, new_gain_second)


def solution(mesh):
    in_specs = (
        P("rep", "grp", None),
        P("rep", None, "grp"),
        P("grp", None),
        P("grp", None),
        P("grp", None),
        P("grp", None),
        P(None, "grp"),
        P(None, "grp"),
        P(None, "grp"),
    )
    out_specs = (
        P("grp", None),
        P("grp", None),
        P("grp", None),
        P("grp", None),
        P(None, "grp"),
        P(None, "grp"),
        P(None, "grp"),
    )
    return jax.shard_map(body, mesh=mesh, in_specs=in_specs, out_specs=out_specs, check_vma=False)
```

```python
import functools

import jax
import jax.numpy as jnp
from jax import lax
from jax.experimental import pallas as pl
from jax.experimental.pallas import tpu as pltpu
from jax.sharding import PartitionSpec as P

beta_first = 0.9
beta_second = 0.999
learn_rate = 0.1
galore_scale = 0.25
adam_eps = 1e-08

CHIPS = 64
ROWS = 8
NCOL = 9216
OWN = NCOL // CHIPS
RANK = 256
LANE = 128
PIECE = 16
BLOCK = 25
MAIN, LOW, HIGH = (slice(at, at + 8) for at in (1, 9, 17))
VMEM_LIMIT = 16 * 1024 * 1024

SWAP = [(0, 1), (1, 0)]


def dot(left, right, left_dim, right_dim):
    return lax.dot_general(
        left,
        right,
        (((left_dim,), (right_dim,)), ((), ())),
        precision=lax.Precision.HIGHEST,
        preferred_element_type=jnp.float32,
    )


def split(value):
    high = value.astype(jnp.bfloat16)
    return high, (value - high.astype(jnp.float32)).astype(jnp.bfloat16)


def split_dot(left, right, left_dim, right_dim):
    def one(a, b):
        return lax.dot_general(
            a, b, (((left_dim,), (right_dim,)), ((), ())), preferred_element_type=jnp.float32
        )

    return one(left[0], right[0]) + (one(left[0], right[1]) + one(left[1], right[0]))


def call(kernel, out_shape, scratch=(), **specs):
    return pl.pallas_call(
        kernel,
        out_shape=out_shape,
        **specs,
        scratch_shapes=list(scratch),
        compiler_params=pltpu.CompilerParams(vmem_limit_bytes=VMEM_LIMIT),
    )


def f32(*shape):
    return jax.ShapeDtypeStruct(shape, jnp.float32)


def any_spec():
    return pl.BlockSpec(memory_space=pl.ANY)


def vmem_spec():
    return pl.BlockSpec(memory_space=pltpu.VMEM)


def iota(axis):
    return lax.broadcasted_iota(jnp.int32, (ROWS, LANE), axis)


def half_rows(core):
    return pl.ds(pl.multiple_of(core * ROWS, ROWS), ROWS)


def swap_pieces(tile):
    row, piece = iota(0), iota(1) // PIECE
    for bit in (1, 2, 4):
        up = pltpu.roll(pltpu.roll(tile, ROWS - bit, 0), PIECE * bit, 1)
        down = pltpu.roll(pltpu.roll(tile, bit, 0), LANE - PIECE * bit, 1)
        row_set, piece_set = (row & bit) != 0, (piece & bit) != 0
        tile = jnp.where(row_set == piece_set, tile, jnp.where(piece_set, up, down))
    return tile


def octet(group):
    return pl.ds(BLOCK * 8 * group, 8, stride=BLOCK)


def block_rows(chip, rows):
    return slice(BLOCK * chip + rows.start, BLOCK * chip + rows.stop)


def stage_kernel(grad_ref, basis_ref, gain_ref, grad_out, basis_out, gain_out, gain, sems):
    half = half_rows(lax.axis_index("rep"))
    copies = [
        pltpu.make_async_copy(grad_ref.at[half, :], grad_out, sems.at[0]),
        pltpu.make_async_copy(basis_ref.at[half, :], basis_out, sems.at[1]),
        pltpu.make_async_copy(gain_ref, gain, sems.at[2]),
    ]
    for copy in copies:
        copy.start()
    gain_out[...] = jnp.zeros_like(gain_out)
    for copy in copies:
        copy.wait()
    gain_out[:2, : 2 * ROWS] = gain[...]


def pack_kernel(own_ref, other_ref, basis_ref, out_ref):
    half = half_rows(lax.axis_index("rep"))
    lane, piece = iota(1), iota(1) // PIECE
    low, high = basis_ref[:, :LANE], basis_ref[:, LANE:]
    for group in range(8):
        tiles = []
        for t in range(9):
            cols = pl.ds((9 * group + t) * LANE, LANE)
            tiles.append(own_ref[:, cols] + other_ref[half, cols])
        last = tiles[8]
        for j in range(8):
            chip = 8 * group + j
            out_ref[block_rows(chip, MAIN), :] = jnp.where(
                lane >= PIECE * j, tiles[j], tiles[j + 1]
            )
            out_ref[block_rows(chip, LOW), :] = low
            out_ref[block_rows(chip, HIGH), :] = high
            last = jnp.where(piece == j, tiles[j + 1], last)
        out_ref[octet(group), :] = swap_pieces(last)


def project_kernel(in_ref, grad_ref, basis_ref, out_ref, twice):
    piece = iota(1) // PIECE
    for group in range(8):
        last = swap_pieces(in_ref[octet(group), :])
        for j in range(8):
            chip = 8 * group + j
            rows = slice(ROWS * chip, ROWS * chip + ROWS)
            grad_ref[rows, :LANE] = in_ref[block_rows(chip, MAIN), :]
            grad_ref[rows, LANE:] = jnp.where(piece == j, last, 0.0)
            basis_ref[rows, :LANE] = in_ref[block_rows(chip, LOW), :]
            basis_ref[rows, LANE:] = in_ref[block_rows(chip, HIGH), :]
    product = dot(grad_ref[...], basis_ref[...], 0, 0)
    twice[:LANE, :] = product[:LANE]
    twice[LANE:, :] = product[:LANE]
    first = pl.multiple_of(lax.rem(lax.axis_index("grp"), 8) * PIECE, PIECE)
    out_ref[:LANE, :] = twice[pl.ds(first, LANE), :]
    out_ref[LANE:, :] = sum(
        product[LANE + PIECE * j : LANE + PIECE * (j + 1)] for j in range(8)
    )


def spread_columns(values, twice, out):
    twice[:LANE, :] = values[:LANE]
    twice[LANE:, :] = values[:LANE]
    first = pl.multiple_of(LANE - lax.rem(lax.axis_index("grp"), 8) * PIECE, PIECE)
    out[:LANE, :] = twice[pl.ds(first, LANE), :]
    for j in range(8):
        out[LANE + PIECE * j : LANE + PIECE * (j + 1), :] = values[LANE:]


def adam(value, first, second):
    corr_first = 1.0 - beta_first**10
    corr_second = 1.0 - beta_second**10
    new_first = beta_first * first + (1.0 - beta_first) * value
    new_second = beta_second * second + (1.0 - beta_second) * value * value
    direction = new_first / corr_first / (jnp.sqrt(new_second / corr_second) + adam_eps)
    return new_first, new_second, direction


def subspace_update_kernel(
    grad_ref, basis_ref, own_ref, other_ref, first_ref, second_ref,
    out_ref, twice, projected_wide, direction_wide,
):
    projected = own_ref[...] + other_ref[...]
    _, _, direction = adam(projected, first_ref[...], second_ref[...])
    spread_columns(projected, twice, projected_wide)
    spread_columns(direction, twice, direction_wide)
    subspace = split_dot(split(grad_ref[...]), split(projected_wide[...]), 1, 0)
    update = split_dot(split(basis_ref[...]), split(direction_wide[...]), 1, 1)
    diagonal = iota(0) == iota(1) // PIECE
    for chip in range(CHIPS):
        rows = slice(ROWS * chip, ROWS * chip + ROWS)
        out_ref[block_rows(chip, MAIN), :] = update[rows, :LANE]
        out_ref[block_rows(chip, LOW), :] = subspace[rows, :LANE]
        out_ref[block_rows(chip, HIGH), :] = subspace[rows, LANE:]
        out_ref[BLOCK * chip : BLOCK * chip + 1, :] = jnp.sum(
            jnp.where(diagonal, update[rows, LANE:], 0.0), axis=0, keepdims=True
        )


def subspace_kernel(in_ref, gain_ref, rows_ref, out_ref):
    low = sum(in_ref[block_rows(chip, LOW), :] for chip in range(CHIPS))
    high = sum(in_ref[block_rows(chip, HIGH), :] for chip in range(CHIPS))
    rows = jnp.concatenate([low, high], axis=1)
    rows_ref[:ROWS, :] = rows
    rows_ref[ROWS:, :LANE] = gain_ref[...]
    rows_ref[ROWS:, LANE:] = jnp.zeros((ROWS, LANE), jnp.float32)
    out_ref[...] = jnp.broadcast_to(rows[None], out_ref.shape)


def weights_kernel(
    in_ref, weights_ref, own_ref, other_ref, first_ref, second_ref,
    out_ref, new_first_ref, new_second_ref,
):
    projected = own_ref[...] + other_ref[...]
    new_first_ref[...], new_second_ref[...], _ = adam(projected, first_ref[...], second_ref[...])
    half = half_rows(lax.axis_index("rep"))
    lane = iota(1)
    for group in range(8):
        last = swap_pieces(in_ref[octet(group), :])
        mains = [in_ref[block_rows(8 * group + j, MAIN), :] for j in range(8)]
        for t in range(9):
            update = last
            if t < 8:
                update = jnp.where(lane >= PIECE * t, mains[t], update)
            if t > 0:
                update = jnp.where(lane < PIECE * (t - 1), mains[t - 1], update)
            cols = pl.ds((9 * group + t) * LANE, LANE)
            out_ref[:, cols] = weights_ref[half, cols] - learn_rate * galore_scale * update


def join_kernel(
    own_ref, other_ref, rows_ref, other_rows_ref, gains_ref, gain_first_ref, gain_second_ref,
    out_ref, rows_out, new_gains_ref, new_gain_first_ref, new_gain_second_ref,
):
    core = lax.axis_index("rep")
    out_ref[half_rows(core), :] = own_ref[...]
    out_ref[half_rows(1 - core), :] = other_ref[...]
    rows_out[half_rows(core), :] = rows_ref[:ROWS, :]
    rows_out[half_rows(1 - core), :] = other_rows_ref[:ROWS, :]
    gain = (rows_ref[ROWS:, :] + other_rows_ref[ROWS:, :])[:2, : 2 * ROWS]
    new_first, new_second, direction = adam(gain, gain_first_ref[...], gain_second_ref[...])
    new_gain_first_ref[...] = new_first
    new_gain_second_ref[...] = new_second
    new_gains_ref[...] = gains_ref[...] - learn_rate * direction


def gram_kernel(in_ref, rows_ref, out_ref):
    subspace = split(in_ref[...])
    out_ref[...] = split_dot(subspace, subspace, 0, 0)


def refresh_kernel(own_gram_ref, other_gram_ref, rows_ref, out_ref):
    gram = own_gram_ref[...] + other_gram_ref[...]
    gram_split = split(gram)
    gram_square = split_dot(gram_split, gram_split, 1, 0)
    scale = jnp.sqrt(jnp.sqrt(jnp.sum(gram * gram, keepdims=True) + 1e-06))
    inverse = 1.0 / (scale * scale)
    current = gram * inverse
    square = jnp.where(scale < jnp.inf, gram_square, 0.0) * inverse * inverse
    current_split = split(current)
    iterate = rows_ref[...] / scale
    iterate = 1.5 * iterate - 0.5 * split_dot(split(iterate), current_split, 1, 0)
    current = 2.25 * current + split_dot(
        current_split, split(0.25 * square - 1.5 * current), 1, 0
    )
    current_split = split(current)
    square = split_dot(current_split, current_split, 1, 0)
    iterate = 1.5 * iterate - 0.5 * split_dot(split(iterate), current_split, 1, 0)
    last = split_dot(split(iterate), current_split, 1, 0)
    last = 2.25 * last + split_dot(split(last), split(0.25 * square - 1.5 * current), 1, 0)
    out_ref[...] = 1.5 * iterate - 0.5 * last


def body(
    grad_parts,
    gain_grad_parts,
    weights,
    basis,
    moment_first,
    moment_second,
    gains,
    gain_first,
    gain_second,
):
    swap = functools.partial(lax.ppermute, axis_name="rep", perm=SWAP)
    vmem = pltpu.VMEM
    hbm = functools.partial(pltpu.with_memory_space_constraint, memory_space=pltpu.HBM)

    def exchange(blocks):
        out = lax.all_to_all(blocks, "grp", split_axis=0, concat_axis=0, tiled=True)
        return out

    def exchange_blocks(blocks):
        return exchange(blocks.reshape(CHIPS * BLOCK, 1, LANE)).reshape(CHIPS * BLOCK, LANE)

    wide = f32(CHIPS * ROWS, RANK)
    small = f32(2, 2 * ROWS)
    local_grad = grad_parts[0]
    other_grad = swap(local_grad)
    own_grad, own_basis, gain = call(
        stage_kernel,
        (f32(ROWS, NCOL), f32(ROWS, RANK), f32(ROWS, LANE)),
        [vmem((2, 2 * ROWS), jnp.float32), pltpu.SemaphoreType.DMA((3,))],
        in_specs=[pl.BlockSpec(memory_space=pltpu.HBM)] * 3,
    )(*(hbm(x) for x in (local_grad, basis, gain_grad_parts[0])))
    packed = call(pack_kernel, f32(CHIPS * BLOCK, LANE))(own_grad, other_grad, own_basis)
    columns, full_basis, part = call(
        project_kernel, (wide, wide, f32(OWN, RANK)), [vmem((2 * LANE, RANK), jnp.float32)]
    )(exchange_blocks(packed))
    other_part = swap(part)
    out = call(
        subspace_update_kernel,
        f32(CHIPS * BLOCK, LANE),
        [vmem((2 * LANE, RANK), jnp.float32)] * 3,
    )(columns, full_basis, part, other_part, moment_first, moment_second)
    back = exchange_blocks(out)
    rows, spread = call(
        subspace_kernel, (f32(2 * ROWS, RANK), vmem((CHIPS, ROWS, RANK), jnp.float32))
    )(back, gain)
    subspace = exchange(spread).reshape(CHIPS * ROWS, RANK)
    half, new_first, new_second = call(
        weights_kernel, (f32(ROWS, NCOL), f32(OWN, RANK), f32(OWN, RANK))
    )(back, weights, part, other_part, moment_first, moment_second)
    new_weights, both_rows, new_gains, new_gain_first, new_gain_second = call(
        join_kernel, (f32(2 * ROWS, NCOL), f32(2 * ROWS, RANK), small, small, small)
    )(half, swap(half), rows, swap(rows), gains, gain_first, gain_second)
    gram = call(
        gram_kernel, f32(RANK, RANK), in_specs=[vmem_spec(), any_spec()]
    )(subspace, both_rows)
    new_basis = call(refresh_kernel, f32(2 * ROWS, RANK))(gram, swap(gram), both_rows)
    return (new_weights, new_first, new_second, new_basis, new_gains, new_gain_first, new_gain_second)


def solution(mesh):
    in_specs = (
        P("rep", "grp", None),
        P("rep", None, "grp"),
        P("grp", None),
        P("grp", None),
        P("grp", None),
        P("grp", None),
        P(None, "grp"),
        P(None, "grp"),
        P(None, "grp"),
    )
    out_specs = (
        P("grp", None),
        P("grp", None),
        P("grp", None),
        P("grp", None),
        P(None, "grp"),
        P(None, "grp"),
        P(None, "grp"),
    )
    return jax.shard_map(body, mesh=mesh, in_specs=in_specs, out_specs=out_specs, check_vma=False)
```

```python
import functools

import jax
import jax.numpy as jnp
from jax import lax
from jax.experimental import pallas as pl
from jax.experimental.pallas import tpu as pltpu
from jax.sharding import PartitionSpec as P

beta_first = 0.9
beta_second = 0.999
learn_rate = 0.1
galore_scale = 0.25
adam_eps = 1e-08

CHIPS = 64
ROWS = 8
NCOL = 9216
OWN = NCOL // CHIPS
RANK = 256
LANE = 128
PIECE = 16
BLOCK = 25
MAIN, LOW, HIGH = (slice(at, at + 8) for at in (1, 9, 17))
VMEM_LIMIT = 16 * 1024 * 1024

SWAP = [(0, 1), (1, 0)]


def dot(left, right, left_dim, right_dim):
    return lax.dot_general(
        left,
        right,
        (((left_dim,), (right_dim,)), ((), ())),
        precision=lax.Precision.HIGHEST,
        preferred_element_type=jnp.float32,
    )


def split(value):
    high = value.astype(jnp.bfloat16)
    return high, (value - high.astype(jnp.float32)).astype(jnp.bfloat16)


def split_dot(left, right, left_dim, right_dim):
    def one(a, b):
        return lax.dot_general(
            a, b, (((left_dim,), (right_dim,)), ((), ())), preferred_element_type=jnp.float32
        )

    return one(left[0], right[0]) + (one(left[0], right[1]) + one(left[1], right[0]))


def call(kernel, out_shape, scratch=(), **specs):
    return pl.pallas_call(
        kernel,
        out_shape=out_shape,
        **specs,
        scratch_shapes=list(scratch),
        compiler_params=pltpu.CompilerParams(vmem_limit_bytes=VMEM_LIMIT),
    )


def f32(*shape):
    return jax.ShapeDtypeStruct(shape, jnp.float32)


def any_spec():
    return pl.BlockSpec(memory_space=pl.ANY)


def vmem_spec():
    return pl.BlockSpec(memory_space=pltpu.VMEM)


def iota(axis):
    return lax.broadcasted_iota(jnp.int32, (ROWS, LANE), axis)


def half_rows(core):
    return pl.ds(pl.multiple_of(core * ROWS, ROWS), ROWS)


def swap_pieces(tile):
    row, piece = iota(0), iota(1) // PIECE
    for bit in (1, 2, 4):
        up = pltpu.roll(pltpu.roll(tile, ROWS - bit, 0), PIECE * bit, 1)
        down = pltpu.roll(pltpu.roll(tile, bit, 0), LANE - PIECE * bit, 1)
        row_set, piece_set = (row & bit) != 0, (piece & bit) != 0
        tile = jnp.where(row_set == piece_set, tile, jnp.where(piece_set, up, down))
    return tile


def octet(group):
    return pl.ds(BLOCK * 8 * group, 8, stride=BLOCK)


def block_rows(chip, rows):
    return slice(BLOCK * chip + rows.start, BLOCK * chip + rows.stop)


def stage_kernel(grad_ref, basis_ref, gain_ref, grad_out, basis_out, gain_out, gain, sems):
    half = half_rows(lax.axis_index("rep"))
    copies = [
        pltpu.make_async_copy(grad_ref.at[half, :], grad_out, sems.at[0]),
        pltpu.make_async_copy(basis_ref.at[half, :], basis_out, sems.at[1]),
        pltpu.make_async_copy(gain_ref, gain, sems.at[2]),
    ]
    for copy in copies:
        copy.start()
    gain_out[...] = jnp.zeros_like(gain_out)
    for copy in copies:
        copy.wait()
    gain_out[:2, : 2 * ROWS] = gain[...]


def pack_kernel(own_ref, other_ref, basis_ref, out_ref):
    half = half_rows(lax.axis_index("rep"))
    lane, piece = iota(1), iota(1) // PIECE
    low, high = basis_ref[:, :LANE], basis_ref[:, LANE:]
    for group in range(8):
        tiles = []
        for t in range(9):
            cols = pl.ds((9 * group + t) * LANE, LANE)
            tiles.append(own_ref[:, cols] + other_ref[half, cols])
        last = tiles[8]
        for j in range(8):
            chip = 8 * group + j
            out_ref[block_rows(chip, MAIN), :] = jnp.where(
                lane >= PIECE * j, tiles[j], tiles[j + 1]
            )
            out_ref[block_rows(chip, LOW), :] = low
            out_ref[block_rows(chip, HIGH), :] = high
            last = jnp.where(piece == j, tiles[j + 1], last)
        out_ref[octet(group), :] = swap_pieces(last)


def project_kernel(in_ref, grad_ref, basis_ref, out_ref, twice):
    for group in range(8):
        last = swap_pieces(in_ref[octet(group), :])
        for j in range(8):
            chip = 8 * group + j
            rows = slice(ROWS * chip, ROWS * chip + ROWS)
            grad_ref[rows, :LANE] = in_ref[block_rows(chip, MAIN), :]
            grad_ref[rows, LANE:] = pltpu.roll(last, LANE - PIECE * j, 1) if j else last
            basis_ref[rows, :LANE] = in_ref[block_rows(chip, LOW), :]
            basis_ref[rows, LANE:] = in_ref[block_rows(chip, HIGH), :]
    product = dot(grad_ref[:, :OWN], basis_ref[...], 0, 0)
    twice[:LANE, :] = product[:LANE]
    twice[LANE:, :] = product[:LANE]
    first = pl.multiple_of(lax.rem(lax.axis_index("grp"), 8) * PIECE, PIECE)
    out_ref[:LANE, :] = twice[pl.ds(first, LANE), :]
    out_ref[LANE:, :] = product[LANE:]


def spread_columns(values, twice, out):
    twice[:LANE, :] = values[:LANE]
    twice[LANE:, :] = values[:LANE]
    first = pl.multiple_of(LANE - lax.rem(lax.axis_index("grp"), 8) * PIECE, PIECE)
    out[:LANE, :] = twice[pl.ds(first, LANE), :]
    for j in range(8):
        out[LANE + PIECE * j : LANE + PIECE * (j + 1), :] = values[LANE:]


def adam(value, first, second):
    corr_first = 1.0 - beta_first**10
    corr_second = 1.0 - beta_second**10
    new_first = beta_first * first + (1.0 - beta_first) * value
    new_second = beta_second * second + (1.0 - beta_second) * value * value
    direction = new_first / corr_first / (jnp.sqrt(new_second / corr_second) + adam_eps)
    return new_first, new_second, direction


def subspace_update_kernel(
    grad_ref, basis_ref, own_ref, other_ref, first_ref, second_ref,
    out_ref, twice, projected_wide, direction_wide,
):
    projected = own_ref[...] + other_ref[...]
    _, _, direction = adam(projected, first_ref[...], second_ref[...])
    spread_columns(projected, twice, projected_wide)
    spread_columns(direction, twice, direction_wide)
    subspace = split_dot(split(grad_ref[:, :OWN]), split(projected_wide[:OWN, :]), 1, 0)
    update = split_dot(split(basis_ref[...]), split(direction_wide[...]), 1, 1)
    diagonal = iota(0) == iota(1) // PIECE
    for chip in range(CHIPS):
        rows = slice(ROWS * chip, ROWS * chip + ROWS)
        out_ref[block_rows(chip, MAIN), :] = update[rows, :LANE]
        out_ref[block_rows(chip, LOW), :] = subspace[rows, :LANE]
        out_ref[block_rows(chip, HIGH), :] = subspace[rows, LANE:]
        out_ref[BLOCK * chip : BLOCK * chip + 1, :] = jnp.sum(
            jnp.where(diagonal, update[rows, LANE:], 0.0), axis=0, keepdims=True
        )


def subspace_kernel(in_ref, gain_ref, rows_ref, out_ref):
    low = sum(in_ref[block_rows(chip, LOW), :] for chip in range(CHIPS))
    high = sum(in_ref[block_rows(chip, HIGH), :] for chip in range(CHIPS))
    rows = jnp.concatenate([low, high], axis=1)
    rows_ref[:ROWS, :] = rows
    rows_ref[ROWS:, :LANE] = gain_ref[...]
    rows_ref[ROWS:, LANE:] = jnp.zeros((ROWS, LANE), jnp.float32)
    out_ref[...] = jnp.broadcast_to(rows[None], out_ref.shape)


def weights_kernel(
    in_ref, weights_ref, own_ref, other_ref, first_ref, second_ref,
    out_ref, new_first_ref, new_second_ref,
):
    projected = own_ref[...] + other_ref[...]
    new_first_ref[...], new_second_ref[...], _ = adam(projected, first_ref[...], second_ref[...])
    half = half_rows(lax.axis_index("rep"))
    lane = iota(1)
    for group in range(8):
        last = swap_pieces(in_ref[octet(group), :])
        mains = [in_ref[block_rows(8 * group + j, MAIN), :] for j in range(8)]
        for t in range(9):
            update = last
            if t < 8:
                update = jnp.where(lane >= PIECE * t, mains[t], update)
            if t > 0:
                update = jnp.where(lane < PIECE * (t - 1), mains[t - 1], update)
            cols = pl.ds((9 * group + t) * LANE, LANE)
            out_ref[:, cols] = weights_ref[half, cols] - learn_rate * galore_scale * update


def join_kernel(
    own_ref, other_ref, rows_ref, other_rows_ref, gains_ref, gain_first_ref, gain_second_ref,
    out_ref, rows_out, new_gains_ref, new_gain_first_ref, new_gain_second_ref,
):
    core = lax.axis_index("rep")
    out_ref[half_rows(core), :] = own_ref[...]
    out_ref[half_rows(1 - core), :] = other_ref[...]
    rows_out[half_rows(core), :] = rows_ref[:ROWS, :]
    rows_out[half_rows(1 - core), :] = other_rows_ref[:ROWS, :]
    gain = (rows_ref[ROWS:, :] + other_rows_ref[ROWS:, :])[:2, : 2 * ROWS]
    new_first, new_second, direction = adam(gain, gain_first_ref[...], gain_second_ref[...])
    new_gain_first_ref[...] = new_first
    new_gain_second_ref[...] = new_second
    new_gains_ref[...] = gains_ref[...] - learn_rate * direction


def gram_kernel(in_ref, rows_ref, out_ref):
    subspace = split(in_ref[...])
    out_ref[...] = split_dot(subspace, subspace, 0, 0)


def refresh_kernel(own_gram_ref, other_gram_ref, rows_ref, out_ref):
    gram = own_gram_ref[...] + other_gram_ref[...]
    gram_split = split(gram)
    gram_square = split_dot(gram_split, gram_split, 1, 0)
    scale = jnp.sqrt(jnp.sqrt(jnp.sum(gram * gram, keepdims=True) + 1e-06))
    inverse = 1.0 / (scale * scale)
    current = gram * inverse
    square = jnp.where(scale < jnp.inf, gram_square, 0.0) * inverse * inverse
    current_split = split(current)
    iterate = rows_ref[...] / scale
    iterate = 1.5 * iterate - 0.5 * split_dot(split(iterate), current_split, 1, 0)
    current = 2.25 * current + split_dot(
        current_split, split(0.25 * square - 1.5 * current), 1, 0
    )
    current_split = split(current)
    square = split_dot(current_split, current_split, 1, 0)
    iterate = 1.5 * iterate - 0.5 * split_dot(split(iterate), current_split, 1, 0)
    last = split_dot(split(iterate), current_split, 1, 0)
    last = 2.25 * last + split_dot(split(last), split(0.25 * square - 1.5 * current), 1, 0)
    out_ref[...] = 1.5 * iterate - 0.5 * last


def body(
    grad_parts,
    gain_grad_parts,
    weights,
    basis,
    moment_first,
    moment_second,
    gains,
    gain_first,
    gain_second,
):
    swap = functools.partial(lax.ppermute, axis_name="rep", perm=SWAP)
    vmem = pltpu.VMEM
    hbm = functools.partial(pltpu.with_memory_space_constraint, memory_space=pltpu.HBM)

    def exchange(blocks):
        out = lax.all_to_all(blocks, "grp", split_axis=0, concat_axis=0, tiled=True)
        return out

    def exchange_blocks(blocks):
        return exchange(blocks.reshape(CHIPS * BLOCK, 1, LANE)).reshape(CHIPS * BLOCK, LANE)

    wide = f32(CHIPS * ROWS, RANK)
    small = f32(2, 2 * ROWS)
    local_grad = grad_parts[0]
    other_grad = swap(local_grad)
    own_grad, own_basis, gain = call(
        stage_kernel,
        (f32(ROWS, NCOL), f32(ROWS, RANK), f32(ROWS, LANE)),
        [vmem((2, 2 * ROWS), jnp.float32), pltpu.SemaphoreType.DMA((3,))],
        in_specs=[pl.BlockSpec(memory_space=pltpu.HBM)] * 3,
    )(*(hbm(x) for x in (local_grad, basis, gain_grad_parts[0])))
    packed = call(pack_kernel, f32(CHIPS * BLOCK, LANE))(own_grad, other_grad, own_basis)
    columns, full_basis, part = call(
        project_kernel, (wide, wide, f32(OWN, RANK)), [vmem((2 * LANE, RANK), jnp.float32)]
    )(exchange_blocks(packed))
    other_part = swap(part)
    out = call(
        subspace_update_kernel,
        f32(CHIPS * BLOCK, LANE),
        [vmem((2 * LANE, RANK), jnp.float32)] * 3,
    )(columns, full_basis, part, other_part, moment_first, moment_second)
    back = exchange_blocks(out)
    rows, spread = call(
        subspace_kernel, (f32(2 * ROWS, RANK), vmem((CHIPS, ROWS, RANK), jnp.float32))
    )(back, gain)
    subspace = exchange(spread).reshape(CHIPS * ROWS, RANK)
    half, new_first, new_second = call(
        weights_kernel, (f32(ROWS, NCOL), f32(OWN, RANK), f32(OWN, RANK))
    )(back, weights, part, other_part, moment_first, moment_second)
    new_weights, both_rows, new_gains, new_gain_first, new_gain_second = call(
        join_kernel, (f32(2 * ROWS, NCOL), f32(2 * ROWS, RANK), small, small, small)
    )(half, swap(half), rows, swap(rows), gains, gain_first, gain_second)
    gram = call(
        gram_kernel, f32(RANK, RANK), in_specs=[vmem_spec(), any_spec()]
    )(subspace, both_rows)
    new_basis = call(refresh_kernel, f32(2 * ROWS, RANK))(gram, swap(gram), both_rows)
    return (new_weights, new_first, new_second, new_basis, new_gains, new_gain_first, new_gain_second)


def solution(mesh):
    in_specs = (
        P("rep", "grp", None),
        P("rep", None, "grp"),
        P("grp", None),
        P("grp", None),
        P("grp", None),
        P("grp", None),
        P(None, "grp"),
        P(None, "grp"),
        P(None, "grp"),
    )
    out_specs = (
        P("grp", None),
        P("grp", None),
        P("grp", None),
        P("grp", None),
        P(None, "grp"),
        P(None, "grp"),
        P(None, "grp"),
    )
    return jax.shard_map(body, mesh=mesh, in_specs=in_specs, out_specs=out_specs, check_vma=False)
```

```python
import functools

import jax
import jax.numpy as jnp
from jax import lax
from jax.experimental import pallas as pl
from jax.experimental.pallas import tpu as pltpu
from jax.sharding import PartitionSpec as P

beta_first = 0.9
beta_second = 0.999
learn_rate = 0.1
galore_scale = 0.25
adam_eps = 1e-08

CHIPS = 64
ROWS = 8
NCOL = 9216
OWN = NCOL // CHIPS
RANK = 256
LANE = 128
PIECE = 16
BLOCK = 25
MAIN, LOW, HIGH = (slice(at, at + 8) for at in (1, 9, 17))
VMEM_LIMIT = 16 * 1024 * 1024

SWAP = [(0, 1), (1, 0)]


def dot(left, right, left_dim, right_dim):
    return lax.dot_general(
        left,
        right,
        (((left_dim,), (right_dim,)), ((), ())),
        precision=lax.Precision.HIGHEST,
        preferred_element_type=jnp.float32,
    )


def split(value):
    high = value.astype(jnp.bfloat16)
    return high, (value - high.astype(jnp.float32)).astype(jnp.bfloat16)


def split_dot(left, right, left_dim, right_dim):
    def one(a, b):
        return lax.dot_general(
            a, b, (((left_dim,), (right_dim,)), ((), ())), preferred_element_type=jnp.float32
        )

    return one(left[0], right[0]) + (one(left[0], right[1]) + one(left[1], right[0]))


def call(kernel, out_shape, scratch=(), **specs):
    return pl.pallas_call(
        kernel,
        out_shape=out_shape,
        **specs,
        scratch_shapes=list(scratch),
        compiler_params=pltpu.CompilerParams(vmem_limit_bytes=VMEM_LIMIT),
    )


def f32(*shape):
    return jax.ShapeDtypeStruct(shape, jnp.float32)


def any_spec():
    return pl.BlockSpec(memory_space=pl.ANY)


def vmem_spec():
    return pl.BlockSpec(memory_space=pltpu.VMEM)


def iota(axis):
    return lax.broadcasted_iota(jnp.int32, (ROWS, LANE), axis)


def half_rows(core):
    return pl.ds(pl.multiple_of(core * ROWS, ROWS), ROWS)


def swap_pieces(tile):
    row, piece = iota(0), iota(1) // PIECE
    for bit in (1, 2, 4):
        up = pltpu.roll(pltpu.roll(tile, ROWS - bit, 0), PIECE * bit, 1)
        down = pltpu.roll(pltpu.roll(tile, bit, 0), LANE - PIECE * bit, 1)
        row_set, piece_set = (row & bit) != 0, (piece & bit) != 0
        tile = jnp.where(row_set == piece_set, tile, jnp.where(piece_set, up, down))
    return tile


def octet(group):
    return pl.ds(BLOCK * 8 * group, 8, stride=BLOCK)


def block_rows(chip, rows):
    return slice(BLOCK * chip + rows.start, BLOCK * chip + rows.stop)


def stage_kernel(grad_ref, basis_ref, gain_ref, grad_out, basis_out, gain_out, gain, sems):
    half = half_rows(lax.axis_index("rep"))
    copies = [
        pltpu.make_async_copy(grad_ref.at[half, :], grad_out, sems.at[0]),
        pltpu.make_async_copy(basis_ref.at[half, :], basis_out, sems.at[1]),
        pltpu.make_async_copy(gain_ref, gain, sems.at[2]),
    ]
    for copy in copies:
        copy.start()
    gain_out[...] = jnp.zeros_like(gain_out)
    for copy in copies:
        copy.wait()
    gain_out[:2, : 2 * ROWS] = gain[...]


def pack_kernel(own_ref, other_ref, basis_ref, out_ref):
    half = half_rows(lax.axis_index("rep"))
    lane, piece = iota(1), iota(1) // PIECE
    low, high = basis_ref[:, :LANE], basis_ref[:, LANE:]
    for group in range(8):
        tiles = []
        for t in range(9):
            cols = pl.ds((9 * group + t) * LANE, LANE)
            tiles.append(own_ref[:, cols] + other_ref[half, cols])
        last = tiles[8]
        for j in range(8):
            chip = 8 * group + j
            out_ref[block_rows(chip, MAIN), :] = jnp.where(
                lane >= PIECE * j, tiles[j], tiles[j + 1]
            )
            out_ref[block_rows(chip, LOW), :] = low
            out_ref[block_rows(chip, HIGH), :] = high
            last = jnp.where(piece == j, tiles[j + 1], last)
        out_ref[octet(group), :] = swap_pieces(last)


def project_kernel(in_ref, grad_ref, basis_ref, out_ref, twice):
    for group in range(8):
        last = swap_pieces(in_ref[octet(group), :])
        for j in range(8):
            chip = 8 * group + j
            rows = slice(ROWS * chip, ROWS * chip + ROWS)
            grad_ref[rows, :LANE] = in_ref[block_rows(chip, MAIN), :]
            grad_ref[rows, LANE:] = pltpu.roll(last, LANE - PIECE * j, 1) if j else last
            basis_ref[rows, :LANE] = in_ref[block_rows(chip, LOW), :]
            basis_ref[rows, LANE:] = in_ref[block_rows(chip, HIGH), :]
    product = dot(grad_ref[:, :OWN], basis_ref[...], 0, 0)
    twice[:LANE, :] = product[:LANE]
    twice[LANE:, :] = product[:LANE]
    first = pl.multiple_of(lax.rem(lax.axis_index("grp"), 8) * PIECE, PIECE)
    out_ref[:LANE, :] = twice[pl.ds(first, LANE), :]
    out_ref[LANE:, :] = product[LANE:]


def spread_columns(values, twice, out):
    twice[:LANE, :] = values[:LANE]
    twice[LANE:, :] = values[:LANE]
    first = pl.multiple_of(LANE - lax.rem(lax.axis_index("grp"), 8) * PIECE, PIECE)
    out[:LANE, :] = twice[pl.ds(first, LANE), :]
    for j in range(8):
        out[LANE + PIECE * j : LANE + PIECE * (j + 1), :] = values[LANE:]


def adam(value, first, second):
    corr_first = 1.0 - beta_first**10
    corr_second = 1.0 - beta_second**10
    new_first = beta_first * first + (1.0 - beta_first) * value
    new_second = beta_second * second + (1.0 - beta_second) * value * value
    direction = new_first / corr_first / (jnp.sqrt(new_second / corr_second) + adam_eps)
    return new_first, new_second, direction


def subspace_update_kernel(
    grad_ref, basis_ref, own_ref, other_ref, first_ref, second_ref,
    out_ref, twice, projected_wide, direction_wide,
):
    projected = own_ref[...] + other_ref[...]
    _, _, direction = adam(projected, first_ref[...], second_ref[...])
    spread_columns(projected, twice, projected_wide)
    spread_columns(direction, twice, direction_wide)
    subspace = split_dot(split(grad_ref[:, :OWN]), split(projected_wide[:OWN, :]), 1, 0)
    update = split_dot(split(basis_ref[...]), split(direction_wide[...]), 1, 1)
    diagonal = iota(0) == iota(1) // PIECE
    for chip in range(CHIPS):
        rows = slice(ROWS * chip, ROWS * chip + ROWS)
        out_ref[block_rows(chip, MAIN), :] = update[rows, :LANE]
        out_ref[block_rows(chip, LOW), :] = subspace[rows, :LANE]
        out_ref[block_rows(chip, HIGH), :] = subspace[rows, LANE:]
        out_ref[BLOCK * chip : BLOCK * chip + 1, :] = jnp.sum(
            jnp.where(diagonal, update[rows, LANE:], 0.0), axis=0, keepdims=True
        )


def tree_sum(terms):
    while len(terms) > 1:
        terms = [a + b for a, b in zip(terms[::2], terms[1::2])]
    return terms[0]


def subspace_kernel(in_ref, gain_ref, rows_ref, out_ref):
    low = tree_sum([in_ref[block_rows(chip, LOW), :] for chip in range(CHIPS)])
    high = tree_sum([in_ref[block_rows(chip, HIGH), :] for chip in range(CHIPS)])
    rows = jnp.concatenate([low, high], axis=1)
    rows_ref[:ROWS, :] = rows
    rows_ref[ROWS:, :LANE] = gain_ref[...]
    rows_ref[ROWS:, LANE:] = jnp.zeros((ROWS, LANE), jnp.float32)
    out_ref[...] = jnp.broadcast_to(rows[None], out_ref.shape)


def weights_kernel(
    in_ref, weights_ref, own_ref, other_ref, first_ref, second_ref,
    out_ref, new_first_ref, new_second_ref,
):
    projected = own_ref[...] + other_ref[...]
    new_first_ref[...], new_second_ref[...], _ = adam(projected, first_ref[...], second_ref[...])
    half = half_rows(lax.axis_index("rep"))
    lane = iota(1)
    for group in range(8):
        last = swap_pieces(in_ref[octet(group), :])
        mains = [in_ref[block_rows(8 * group + j, MAIN), :] for j in range(8)]
        for t in range(9):
            update = last
            if t < 8:
                update = jnp.where(lane >= PIECE * t, mains[t], update)
            if t > 0:
                update = jnp.where(lane < PIECE * (t - 1), mains[t - 1], update)
            cols = pl.ds((9 * group + t) * LANE, LANE)
            out_ref[:, cols] = weights_ref[half, cols] - learn_rate * galore_scale * update


def join_kernel(
    own_ref, other_ref, rows_ref, other_rows_ref, gains_ref, gain_first_ref, gain_second_ref,
    out_ref, rows_out, new_gains_ref, new_gain_first_ref, new_gain_second_ref,
):
    core = lax.axis_index("rep")
    out_ref[half_rows(core), :] = own_ref[...]
    out_ref[half_rows(1 - core), :] = other_ref[...]
    rows_out[half_rows(core), :] = rows_ref[:ROWS, :]
    rows_out[half_rows(1 - core), :] = other_rows_ref[:ROWS, :]
    gain = (rows_ref[ROWS:, :] + other_rows_ref[ROWS:, :])[:2, : 2 * ROWS]
    new_first, new_second, direction = adam(gain, gain_first_ref[...], gain_second_ref[...])
    new_gain_first_ref[...] = new_first
    new_gain_second_ref[...] = new_second
    new_gains_ref[...] = gains_ref[...] - learn_rate * direction


def gram_kernel(in_ref, rows_ref, out_ref):
    subspace = split(in_ref[...])
    out_ref[...] = split_dot(subspace, subspace, 0, 0)


def refresh_kernel(own_gram_ref, other_gram_ref, rows_ref, out_ref):
    gram = own_gram_ref[...] + other_gram_ref[...]
    gram_split = split(gram)
    gram_square = split_dot(gram_split, gram_split, 1, 0)
    scale = jnp.sqrt(jnp.sqrt(jnp.sum(gram * gram, keepdims=True) + 1e-06))
    inverse = 1.0 / (scale * scale)
    current = gram * inverse
    square = jnp.where(scale < jnp.inf, gram_square, 0.0) * inverse * inverse
    current_split = split(current)
    iterate = rows_ref[...] / scale
    iterate = 1.5 * iterate - 0.5 * split_dot(split(iterate), current_split, 1, 0)
    current = 2.25 * current + split_dot(
        current_split, split(0.25 * square - 1.5 * current), 1, 0
    )
    current_split = split(current)
    square = split_dot(current_split, current_split, 1, 0)
    iterate = 1.5 * iterate - 0.5 * split_dot(split(iterate), current_split, 1, 0)
    last = split_dot(split(iterate), current_split, 1, 0)
    last = 2.25 * last + split_dot(split(last), split(0.25 * square - 1.5 * current), 1, 0)
    out_ref[...] = 1.5 * iterate - 0.5 * last


def body(
    grad_parts,
    gain_grad_parts,
    weights,
    basis,
    moment_first,
    moment_second,
    gains,
    gain_first,
    gain_second,
):
    swap = functools.partial(lax.ppermute, axis_name="rep", perm=SWAP)
    vmem = pltpu.VMEM
    hbm = functools.partial(pltpu.with_memory_space_constraint, memory_space=pltpu.HBM)

    def exchange(blocks):
        out = lax.all_to_all(blocks, "grp", split_axis=0, concat_axis=0, tiled=True)
        return out

    def exchange_blocks(blocks):
        return exchange(blocks.reshape(CHIPS * BLOCK, 1, LANE)).reshape(CHIPS * BLOCK, LANE)

    wide = f32(CHIPS * ROWS, RANK)
    small = f32(2, 2 * ROWS)
    local_grad = grad_parts[0]
    other_grad = swap(local_grad)
    own_grad, own_basis, gain = call(
        stage_kernel,
        (f32(ROWS, NCOL), f32(ROWS, RANK), f32(ROWS, LANE)),
        [vmem((2, 2 * ROWS), jnp.float32), pltpu.SemaphoreType.DMA((3,))],
        in_specs=[pl.BlockSpec(memory_space=pltpu.HBM)] * 3,
    )(*(hbm(x) for x in (local_grad, basis, gain_grad_parts[0])))
    packed = call(pack_kernel, f32(CHIPS * BLOCK, LANE))(own_grad, other_grad, own_basis)
    columns, full_basis, part = call(
        project_kernel, (wide, wide, f32(OWN, RANK)), [vmem((2 * LANE, RANK), jnp.float32)]
    )(exchange_blocks(packed))
    other_part = swap(part)
    out = call(
        subspace_update_kernel,
        f32(CHIPS * BLOCK, LANE),
        [vmem((2 * LANE, RANK), jnp.float32)] * 3,
    )(columns, full_basis, part, other_part, moment_first, moment_second)
    back = exchange_blocks(out)
    rows, spread = call(
        subspace_kernel, (f32(2 * ROWS, RANK), vmem((CHIPS, ROWS, RANK), jnp.float32))
    )(back, gain)
    subspace = exchange(spread).reshape(CHIPS * ROWS, RANK)
    half, new_first, new_second = call(
        weights_kernel, (f32(ROWS, NCOL), f32(OWN, RANK), f32(OWN, RANK))
    )(back, weights, part, other_part, moment_first, moment_second)
    new_weights, both_rows, new_gains, new_gain_first, new_gain_second = call(
        join_kernel, (f32(2 * ROWS, NCOL), f32(2 * ROWS, RANK), small, small, small)
    )(half, swap(half), rows, swap(rows), gains, gain_first, gain_second)
    gram = call(
        gram_kernel, f32(RANK, RANK), in_specs=[vmem_spec(), any_spec()]
    )(subspace, both_rows)
    new_basis = call(refresh_kernel, f32(2 * ROWS, RANK))(gram, swap(gram), both_rows)
    return (new_weights, new_first, new_second, new_basis, new_gains, new_gain_first, new_gain_second)


def solution(mesh):
    in_specs = (
        P("rep", "grp", None),
        P("rep", None, "grp"),
        P("grp", None),
        P("grp", None),
        P("grp", None),
        P("grp", None),
        P(None, "grp"),
        P(None, "grp"),
        P(None, "grp"),
    )
    out_specs = (
        P("grp", None),
        P("grp", None),
        P("grp", None),
        P("grp", None),
        P(None, "grp"),
        P(None, "grp"),
        P(None, "grp"),
    )
    return jax.shard_map(body, mesh=mesh, in_specs=in_specs, out_specs=out_specs, check_vma=False)
```
